256 devices in a mesh: sub: 64 (over z, x, core), face: 4 (over y).
Axes of the slice: x: 4, y: 4, z: 8, core: 2. Of those that a mesh axis runs over, the one named last changes fastest.
Arguments:
- own_block: bfloat16 [1024, 512, 512], P(('sub', 'face')), may hold values from -1 to 4, as said below
- own_coupling: bfloat16 [1024, 512, 512], P(('sub', 'face')), may hold values from -0.125 to 0.125
- lent_block: bfloat16 [1024, 512, 512], P(('sub', 'face')), may hold values from -1 to 4, as said below
- lent_coupling: bfloat16 [1024, 512, 512], P(('sub', 'face')), may hold values from -0.125 to 0.125
- face_list: int32 [1024, 2], replicated, may hold values from 0 to 63, as said below
- eig_counts: int32 [1024], P('sub'), may hold values from 1 to 32, as said below
- owner_map: int32 [1024, 1], replicated, may hold values from 0 to 63, as said below
- start_block: float32 [1024, 32, 512], P('sub', None, 'face'), may hold values from -6 to 6
Outputs:
- basis_rows: float32 [1024, 32, 512], P('sub', None, 'face')
- coarse: float32 [1024, 1024], P('sub', 'face')
The draws below stay inside these ranges and needn't reach their ends.
Inputs may be any that keep to these rules, and one draw needn't show every extreme that they name: `face_list`: face f, held by subdomain i = f // 16, pairs with subdomain (i + d) mod 64 for a distance d of 1 to 4; every lent slot of every subdomain is named by exactly one face; the lent slot lies in the same group of 4 slots as the face's own slot (f mod 16) // 4; every subdomain has the same number of faces at each distance, one distance holds exactly 8 of them and no distance more, and some face has distance 4. `eig_counts`: the counts 1 and 32 both occur. `owner_map`: face f of subdomain s = f // 16 has owner (s + d * 16) mod 64 for some d from 0 to 3, and exactly 4 faces of s have each of these 4 owners. `own_block`: symmetric; diagonal entries between 2 and 4. `lent_block`: symmetric; diagonal entries between 2 and 4.
All inputs are finite; a program needn't handle non-finite values.
Results may differ from the reference program's by a relative error of at most 0.0049.
Values may be sent and summed in bfloat16 or wider, within the bound.
A program may use at most 192 MiB of HBM per device.

```python
import jax
import jax.numpy as jnp
from jax import lax

NF = 512
NI = 512
K = 32
ITERS = 3
FPD = 16
REACH = 4
MAXD = 8
CAP = 4
SUBS = 64
FACES = 1024
FPG = 4


def symmetric_field(noise_field, diagonal):
    off_part = (noise_field + jnp.swapaxes(noise_field, 1, 2)) * (0.35 / NF ** 0.5)
    index_range = jnp.arange(NF, dtype=jnp.float32)
    distance = jnp.abs(index_range[:, None] - index_range[None, :])
    length = max(NF // 8, 1) * 1.0
    height = min(10.0 / length, 0.25)
    smooth_part = height * jnp.exp(-distance / length)
    identity = jnp.eye(NF, dtype=jnp.float32)
    return (off_part + smooth_part[None, :, :]) * (1.0 - identity) + identity * diagonal[:, :, None]


def draw_own_block(key, part):
    key = jax.random.fold_in(key, 3)
    first_key, second_key = jax.random.split(key)
    noise_field = jax.random.normal(first_key, (FACES, NF, NF), jnp.float32)
    diagonal = jax.random.uniform(second_key, (FACES, NF), jnp.float32, 2.0, 4.0)
    return symmetric_field(noise_field, diagonal).astype(jnp.bfloat16)


def draw_lent_block(key, part):
    key = jax.random.fold_in(key, 4)
    first_key, second_key = jax.random.split(key)
    noise_field = jax.random.normal(first_key, (FACES, NF, NF), jnp.float32)
    diagonal = jax.random.uniform(second_key, (FACES, NF), jnp.float32, 2.0, 4.0)
    return symmetric_field(noise_field, diagonal).astype(jnp.bfloat16)


def draw_face_list(key, part):
    key = jax.random.fold_in(key, 7)
    subkeys = jax.random.split(key, 5)
    common = jax.random.randint(subkeys[0], (), 1, REACH + 1)
    others = (common - 1 + jax.random.randint(subkeys[1], (FPD - MAXD,), 1, REACH)) % REACH + 1
    others = others.at[0].set(jnp.where(common == REACH, others[0], REACH))
    distances = jnp.concatenate([jnp.full((MAXD,), common, jnp.int32), others.astype(jnp.int32)])
    distances = distances[jax.random.permutation(subkeys[4], FPD)].astype(jnp.int32)
    slot_range = jnp.arange(FPD, dtype=jnp.int32)
    group_score = slot_range // FPG * (1 << 26)
    lend_score = group_score[None, :] + jax.random.randint(subkeys[2], (SUBS, FPD), 0, 1 << 20) * FPD + slot_range[None, :]
    lend_perm = jnp.argsort(lend_score, axis=1).astype(jnp.int32)
    home_score = group_score[None, :] + jax.random.randint(subkeys[3], (SUBS, FPD), 0, 1 << 20) * FPD + slot_range[None, :]
    home_perm = jnp.argsort(home_score, axis=1).astype(jnp.int32)
    home_index = jnp.arange(SUBS, dtype=jnp.int32)[:, None]
    partner = (home_index + distances[None, :]) % SUBS
    lent_slot = lend_perm[partner, slot_range[None, :]]
    table_rows = (home_index * FPD + home_perm).reshape(-1)
    entries = jnp.stack([partner, lent_slot], axis=-1).reshape(SUBS * FPD, 2)
    face_table = jnp.zeros((SUBS * FPD, 2), jnp.int32).at[table_rows].set(entries)
    return face_table.astype(jnp.int32)


def draw_eig_counts(key, part):
    key = jax.random.fold_in(key, 5)
    subkeys = jax.random.split(key, 3)
    counts = jax.random.randint(subkeys[0], (FACES,), 1, K + 1)
    top_index = jax.random.randint(subkeys[1], (), 0, FACES)
    low_index = (top_index + jax.random.randint(subkeys[2], (), 1, FACES)) % FACES
    counts = counts.at[top_index].set(K).at[low_index].set(1)
    return counts.astype(jnp.int32)


def draw_owner_map(key, part):
    key = jax.random.fold_in(key, 9)
    first_key, second_key = jax.random.split(key)
    owner_groups = FPD // CAP
    spacing = SUBS // owner_groups
    slot_range = jnp.arange(FPD, dtype=jnp.int32)
    slot_score = jax.random.randint(first_key, (SUBS, FPD), 0, 1 << 20) * FPD + slot_range[None, :]
    slot_order = jnp.argsort(slot_score, axis=1).astype(jnp.int32)
    group_range = jnp.arange(owner_groups, dtype=jnp.int32)
    group_score = jax.random.randint(second_key, (SUBS, owner_groups), 0, 1 << 20) * owner_groups + group_range[None, :]
    group_order = jnp.argsort(group_score, axis=1).astype(jnp.int32)
    position_distance = group_order[:, slot_range // CAP]
    sub_range = jnp.arange(SUBS, dtype=jnp.int32)[:, None]
    slot_distance = jnp.zeros((SUBS, FPD), jnp.int32).at[sub_range, slot_order].set(position_distance)
    owners = (sub_range + slot_distance * spacing) % SUBS
    return owners.reshape(FACES, 1).astype(jnp.int32)


def level_of(stream_key, extent, pieces, low, top_value):
    factor_of, own = 1.0, jax.random.fold_in(stream_key, 6)
    for axis_at, blocks in pieces:
        steps = jnp.exp(jax.random.uniform(jax.random.fold_in(own, axis_at), (blocks,), jnp.float32, low / len(pieces), top_value / len(pieces)))
        factor_of = factor_of * jnp.repeat(steps, extent[axis_at] // blocks).reshape([-1 if axis == axis_at else 1 for axis in range(len(extent))])
    return factor_of


def gaussian(rng, extent, width, reach, pieces=(), kind=jnp.bfloat16):
    drawn = jax.random.normal(rng, extent, jnp.float32) * width
    if len(pieces) > 0:
        drawn = level_of(rng, extent, pieces, -0.22, 0.18) * drawn
    return jnp.clip(drawn, min=-reach, max=reach).astype(kind)


def setup_inputs(seed: int = 0) -> dict:
    seeds = jax.random.split(jax.random.key(seed), 9)
    own_block = draw_own_block(jax.random.fold_in(seeds[8], 71), 0)
    own_coupling = gaussian(seeds[1], (FACES, NI, NF), ((NI + NF) * 5 // 2) ** -0.5, 0.125, ((0, 256),))
    lent_block = draw_lent_block(jax.random.fold_in(seeds[8], 71), 0)
    lent_coupling = gaussian(seeds[3], (FACES, NI, NF), ((NI + NF) * 5 // 2) ** -0.5, 0.125, ((0, 256),))
    face_list = draw_face_list(jax.random.fold_in(seeds[8], 71), 0)
    eig_counts = draw_eig_counts(jax.random.fold_in(seeds[8], 71), 0)
    owner_map = draw_owner_map(jax.random.fold_in(seeds[8], 71), 0)
    start_block = gaussian(seeds[7], (FACES, K, NF), 1.0, 6.0, ((0, 64), (2, 4)), jnp.float32)
    return {"own_block": own_block, "own_coupling": own_coupling, "lent_block": lent_block, "lent_coupling": lent_coupling, "face_list": face_list, "eig_counts": eig_counts, "owner_map": owner_map, "start_block": start_block}


HIGHEST = lax.Precision.HIGHEST

def face_schur(pair_arrays):
    face_block, coupling = pair_arrays
    product = jnp.dot(coupling.T.astype(jnp.float32), coupling.astype(jnp.float32), preferred_element_type=jnp.float32)
    return (face_block.astype(jnp.float32) - product).astype(jnp.bfloat16)

def reference(own_block, own_coupling, lent_block, lent_coupling, face_list, eig_counts, owner_map, start_block):
    own_schur = lax.map(face_schur, (own_block, own_coupling))
    lent_schur = lax.map(face_schur, (lent_block, lent_coupling))
    own_weight = jnp.diagonal(own_block, axis1=1, axis2=2).astype(jnp.float32)
    lent_weight = jnp.diagonal(lent_block, axis1=1, axis2=2).astype(jnp.float32)
    partner_index = (face_list[:, 0] * FPD + face_list[:, 1]).astype(jnp.int32)

    def solve_face(face_index):
        partner_at = partner_index[face_index]
        operator = own_schur[face_index].astype(jnp.float32) + lent_schur[partner_at].astype(jnp.float32)
        weight = own_weight[face_index] + lent_weight[partner_at]
        iterate = start_block[face_index]
        for sweep_index in range(ITERS):
            image_rows = jnp.dot(iterate, operator.T, precision=HIGHEST) / weight
            gram_matrix = jnp.dot(image_rows * weight, image_rows.T, precision=HIGHEST)
            lower_factor = jnp.linalg.cholesky(gram_matrix)
            iterate = jax.scipy.linalg.solve_triangular(lower_factor, image_rows, lower=True)
        applied = jnp.dot(iterate, operator.T, precision=HIGHEST)
        coarse_block = jnp.dot(iterate, applied.T, precision=HIGHEST)
        kept = (jnp.arange(K, dtype=jnp.int32) < eig_counts[face_index]).astype(jnp.float32)
        masked = coarse_block * kept[:, None] * kept[None, :]
        return (iterate * kept[:, None], masked.reshape(K * K))
    basis_rows, blocks = lax.map(solve_face, jnp.arange(FACES, dtype=jnp.int32))
    owners = owner_map[:, 0].astype(jnp.int32)
    one_hot = (owners[:, None] == jnp.arange(SUBS, dtype=jnp.int32)[None, :]).astype(jnp.int32)
    before = (jnp.cumsum(one_hot, axis=0) - one_hot).astype(jnp.int32)
    rank_among = jnp.sum(before * one_hot, axis=1).astype(jnp.int32)
    row_index = (owners * FPD + rank_among).astype(jnp.int32)
    coarse = jnp.zeros((FACES, K * K), jnp.float32).at[row_index].set(blocks)
    return (basis_rows, coarse)
```

```python
import functools

import jax
import jax.numpy as jnp
from jax import lax
from jax.experimental import pallas as pl
from jax.experimental.pallas import tpu as pltpu
from jax.sharding import PartitionSpec as P

ITERS = 3
REACH = 4
RING = 4
PLUS = (0, 1)

HIGHEST = lax.Precision.HIGHEST
MESH = pl.DeviceIdType.MESH
F32 = jnp.float32
BF16 = jnp.bfloat16


def iota(shape, dim):
    return lax.broadcasted_iota(jnp.int32, shape, dim)


def dot(a, b, ca, cb, precision=None):
    return lax.dot_general(
        a, b, (((ca,), (cb,)), ((), ())), precision=precision, preferred_element_type=F32
    )


def pack_lent(block, coupling, out_ref):
    n = block.shape[0]
    h = n // 2
    c0, c1 = coupling[:, :h], coupling[:, h:]
    b00 = block[:h, :h].astype(F32)
    b11 = block[h:, h:].astype(F32)
    row, col = iota((h, h), 0), iota((h, h), 1)
    out_ref[0:h, :] = (block[:h, h:].astype(F32) - dot(c0, c1, 0, 0)).astype(BF16)
    s00 = b00 - dot(c0, c0, 0, 0)
    s11 = b11 - dot(c1, c1, 0, 0)
    out_ref[h : 2 * h, :] = jnp.where(row <= col, s00, s11).astype(BF16)
    eye = row == col
    diagonals = [jnp.sum(jnp.where(eye, v, 0.0), axis=0, keepdims=True) for v in (s11, b00, b11)]
    at = iota((16, h), 0)
    aux = jnp.where(at == 0, diagonals[0], jnp.where(at == 1, diagonals[1], diagonals[2]))
    out_ref[2 * h :, :] = aux.astype(BF16)


def unpack_lent(packed, out_ref):
    h = packed.shape[1]
    upper = packed[0:h]
    mixed = packed[h : 2 * h].astype(F32)
    aux = packed[2 * h :].astype(F32)
    flipped = mixed.T
    row, col = iota((h, h), 0), iota((h, h), 1)
    out_ref[:h, :h] = jnp.where(row <= col, mixed, flipped).astype(BF16)
    out_ref[h:, h:] = jnp.where(
        row > col, mixed, jnp.where(row < col, flipped, aux[0:1])
    ).astype(BF16)
    out_ref[:h, h:] = upper
    out_ref[h:, :h] = upper.astype(F32).T.astype(BF16)
    return jnp.concatenate([aux[1:2], aux[2:3]], axis=1)


def kernel(
    subs,
    parts,
    own_block,
    own_coupling,
    lent_block,
    lent_coupling,
    start_block,
    owners_ref,
    meta,
    basis,
    coarse,
    lent_b,
    lent_c,
    own_b,
    own_c,
    own_s,
    lent_s,
    tx,
    rx,
    passing,
    x0,
    basis_tx,
    cand_tx,
    cand,
    load_sem,
    x0_local_sem,
    lane1_send,
    lane1_recv,
    mid_send,
    mid_recv,
    lane2_send,
    lane2_recv,
    near_send,
    near_recv,
    far_send,
    far_recv,
    x0_send,
    x0_recv,
    basis_send,
    basis_recv,
    cand_send,
    cand_recv,
):
    faces = own_b.shape[0]
    n = own_b.shape[1]
    k = start_block.shape[1]
    width = start_block.shape[2]
    me = lax.axis_index("sub")
    part = lax.axis_index("face")
    core = lax.rem(me, 2)
    x = lax.rem(me // 2, RING)
    line = me - 2 * x - core
    ahead = line + 2 * lax.rem(x + 1, RING) + core
    behind = line + 2 * lax.rem(x + RING - 1, RING) + core
    spacing = subs // 4
    residue = lax.rem(me, spacing)
    turn = me // spacing

    def around(s):
        return lax.rem(s + 2 * subs, subs)

    other = me + 1 - 2 * core
    down = around(me - 2)
    up = around(me + 2)
    onward = around(behind - 4)
    top = around(me + 4)
    top_core = lax.rem(top, 2)
    top_x = lax.rem(top // 2, RING)
    feeder = top - 2 * top_x + 2 * lax.rem(top_x + 1, RING)

    loads = []
    for f in range(faces):
        for a, (src, dst) in enumerate(((lent_coupling, lent_c), (lent_block, lent_b))):
            loads.append(pltpu.make_async_copy(src.at[f], dst.at[f], load_sem.at[a, f]))
    for f in range(faces):
        for a, (src, dst) in enumerate(((own_coupling, own_c), (own_block, own_b))):
            loads.append(pltpu.make_async_copy(src.at[f], dst.at[f], load_sem.at[a + 2, f]))
    for copy in loads:
        copy.start()
    x0_local = pltpu.make_async_copy(
        start_block.at[pl.ds(part * faces, faces)], x0.at[part], x0_local_sem
    )
    x0_local.start()

    def remote(src, dst, send, recv, s, p):
        return pltpu.make_async_remote_copy(
            src_ref=src,
            dst_ref=dst,
            send_sem=send,
            recv_sem=recv,
            device_id=(s, p),
            device_id_type=MESH,
        )

    barrier = pltpu.get_barrier_semaphore()
    greeted = [(s, part) for s in (down, up, ahead, behind, onward, feeder, other)]
    peers = []
    for dk in range(4):
        for dp in range(parts):
            if dk or dp:
                s = residue + spacing * lax.rem(turn + dk, 4)
                p = lax.rem(part + dp, parts)
                peers.append((dk, dp, s, p))
                greeted.append((s, p))
    for s, p in greeted:
        pl.semaphore_signal(barrier, inc=1, device_id=(s, p), device_id_type=MESH)
    pl.semaphore_wait(barrier, len(greeted))

    x0_copies = []
    for dp in range(1, parts):
        p = lax.rem(part + dp, parts)
        x0_copies.append(
            remote(
                start_block.at[pl.ds(p * faces, faces)],
                x0.at[part],
                x0_send.at[dp - 1],
                x0_recv.at[dp - 1],
                me,
                p,
            )
        )
    lane1 = [
        remote(tx.at[f], rx.at[faces + f], lane1_send.at[f], lane1_recv.at[f], down, part)
        for f in range(faces)
    ]
    mid = [
        remote(tx.at[f], passing.at[i], mid_send.at[i], mid_recv.at[i], ahead, part)
        for i, f in enumerate(PLUS)
    ]
    lane2 = []
    for f in range(faces):
        if f in PLUS:
            src, s = passing.at[PLUS.index(f)], onward
        else:
            src, s = rx.at[faces + f], down
        lane2.append(
            remote(src, rx.at[3 * faces + f], lane2_send.at[f], lane2_recv.at[f], s, part)
        )

    def near(f, src):
        return remote(src, rx.at[f], near_send.at[f], near_recv.at[f], other, part)

    def far(f, src):
        return remote(src, rx.at[2 * faces + f], far_send.at[f], far_recv.at[f], other, part)

    for f in range(faces):
        loads[2 * f].wait()
        loads[2 * f + 1].wait()
        pack_lent(lent_b[f], lent_c[f], tx.at[f])
        lane1[f].start()
        if f in PLUS:
            mid[PLUS.index(f)].start()

        @pl.when(core == 1)
        def _():
            near(f, tx.at[f]).start()

    for copy in x0_copies:
        copy.start()

    own_weights = []
    eye = iota((n, n), 0) == iota((n, n), 1)
    for f in range(faces):
        loads[2 * faces + 2 * f].wait()
        loads[2 * faces + 2 * f + 1].wait()
        coupling = own_c[f]
        block = own_b[f].astype(F32)
        own_s[f] = (block - dot(coupling, coupling, 0, 0)).astype(BF16)
        own_weights.append(jnp.sum(jnp.where(eye, block, 0.0), axis=0, keepdims=True))
        lane1[f].wait_recv()
        if f not in PLUS:
            lane2[f].start()

        @pl.when(core == 0)
        def _():
            near(f, rx.at[faces + f]).start()

        @pl.when(core == 1)
        def _():
            far(f, rx.at[faces + f]).start()

        if f in PLUS:
            mid[PLUS.index(f)].wait_recv()
            lane2[f].start()

    x0_local.wait()
    for copy in x0_copies:
        copy.wait_recv()
    iterate = jnp.concatenate([x0[p].reshape(faces * k, width) for p in range(parts)], axis=1)

    def split(value):
        high = value.astype(BF16)
        return high, (value - high.astype(F32)).astype(BF16)

    def face_rows(value, f):
        return value[f * k : (f + 1) * k]

    def apply(value, tables):
        high, low = split(value)
        out = []
        for f in range(faces):
            stacked = jnp.concatenate([face_rows(high, f), face_rows(low, f)], axis=0)
            got = sum(dot(stacked, table[f], 1, 0) for table in tables)
            out.append(got[:k] + got[k:])
        return jnp.concatenate(out, axis=0)

    applied = apply(iterate, (own_s,))

    for f in range(faces):
        lane2[f].wait_recv()

        @pl.when(core == 0)
        def _():
            far(f, rx.at[3 * faces + f]).start()

    for f in range(faces):
        near(f, tx.at[f]).wait_recv()
        far(f, tx.at[f]).wait_recv()

    weight_rows = []
    for f in range(faces):
        lent_weight = unpack_lent(rx[meta[f]], lent_s.at[f])
        weight_rows.append(own_weights[f] + lent_weight)
    weight = jnp.concatenate([jnp.broadcast_to(w, (k, n)) for w in weight_rows], axis=0)

    rows = faces * k
    lane_face = iota((rows, rows), 1) // k
    same_face = iota((rows, rows), 0) // k == lane_face
    side = (k, rows)
    row_at, lane_at = iota(side, 0), iota(side, 1)
    lane_base = lane_at // k * k

    def orthonormal(applied, image):
        gram = jnp.where(same_face, dot(applied, image, 1, 1, HIGHEST), 0.0)
        gram = sum(face_rows(gram, f) for f in range(faces))
        inverse = jnp.where(row_at == lane_at - lane_base, 1.0, 0.0)
        pivots = jnp.ones(side, F32)
        for j in range(k):
            column = jnp.take_along_axis(gram, lane_base + j, axis=1, mode="promise_in_bounds")
            pivot = column[j : j + 1]
            factor = jnp.where(row_at > j, column / pivot, 0.0)
            pivots = jnp.where(row_at == j, pivot, pivots)
            gram = gram - factor * gram[j : j + 1]
            inverse = inverse - factor * inverse[j : j + 1]
        inverse = inverse * lax.rsqrt(pivots)
        spread = jnp.where(same_face, jnp.concatenate([inverse] * faces, axis=0), 0.0)
        return dot(spread, image, 1, 0, HIGHEST)

    for sweep in range(ITERS):
        if sweep == 0:
            applied = applied + apply(iterate, (lent_s,))
        else:
            applied = apply(iterate, (own_s, lent_s))
        image = applied / weight
        iterate = orthonormal(applied, image)

    face_of_row = iota((rows, 1), 0) // k
    counts = jnp.zeros((rows, 1), jnp.int32)
    for f in range(faces):
        counts = jnp.where(face_of_row == f, meta[faces + f], counts)
    kept_row = iota((rows, 1), 0) - face_of_row * k < counts
    basis_rows = jnp.where(kept_row, iterate, 0.0)
    for p in range(parts):
        basis_tx[p] = basis_rows[:, p * width : (p + 1) * width].reshape(faces, k, width)
    basis_copies = []
    for dp in range(1, parts):
        p = lax.rem(part + dp, parts)
        basis_copies.append(
            remote(
                basis_tx.at[p],
                basis.at[pl.ds(part * faces, faces)],
                basis_send.at[dp - 1],
                basis_recv.at[dp - 1],
                me,
                p,
            )
        )
    for copy in basis_copies:
        copy.start()
    basis_local = pltpu.make_async_copy(
        basis_tx.at[part], basis.at[pl.ds(part * faces, faces)], x0_local_sem
    )
    basis_local.start()

    applied = apply(iterate, (own_s, lent_s))
    block = dot(iterate, applied, 1, 1, HIGHEST)
    lane_kept = iota((rows, rows), 1) - lane_face * k < counts
    block = jnp.where(same_face & kept_row & lane_kept, block, 0.0)
    per_row = rows // k
    repeat = (iota((rows, rows), 0) % k == iota((rows, rows), 1) % k).astype(F32)
    block = dot(block, repeat, 1, 0, HIGHEST)
    block = jnp.where(iota((rows, rows), 0) % per_row == lane_face, block, 0.0)
    halves = k // per_row // parts
    fold_rows = parts * faces * halves
    fold_at, from_at = iota((fold_rows, rows), 0), iota((fold_rows, rows), 1)
    wanted_row = (
        fold_at // halves % faces * k
        + (fold_at // (halves * faces) * halves + fold_at % halves) * per_row
    )
    fold = (from_at // per_row * per_row == wanted_row).astype(F32)
    folded = dot(fold, block, 1, 0, HIGHEST)
    group = faces * halves
    for p in range(parts):
        cand_tx[p] = folded[p * group : (p + 1) * group]
    source = turn * parts + part
    cand_copies = []
    for i, (dk, dp, s, p) in enumerate(peers):
        cand_copies.append(
            remote(cand_tx.at[p], cand.at[source], cand_send.at[i], cand_recv.at[i], s, p)
        )
    for copy in cand_copies:
        copy.start()
    cand[source] = cand_tx[part]

    total = 4 * parts * group
    wanted = (owners_ref[...] == me).astype(F32)
    before_at, after_at = iota((total, total), 0), iota((total, total), 1)
    before = (
        (before_at % halves == 0) & (before_at // halves < after_at // halves)
    ).astype(F32)
    rank = dot(jnp.broadcast_to(wanted, (8, total)), before, 1, 0)[0:1]
    out_rows = coarse.shape[0]
    out_at, cand_at = iota((out_rows, total), 0), iota((out_rows, total), 1)
    chosen = (wanted > 0) & (rank.astype(jnp.int32) == out_at)

    for copy in cand_copies:
        copy.wait_recv()
    candidates = cand[...].reshape(total, rows)
    for h in range(halves):
        choose = jnp.where(chosen & (cand_at % halves == h), 1.0, 0.0)
        coarse[:, h * rows : (h + 1) * rows] = dot(choose, candidates, 1, 0, HIGHEST)

    for copy in basis_copies:
        copy.wait_recv()
    basis_local.wait()
    for copy in lane1 + mid + lane2 + x0_copies + basis_copies + cand_copies:
        copy.wait_send()
    for f in range(faces):
        near(f, tx.at[f]).wait_send()
        far(f, tx.at[f]).wait_send()


def shards(
    subs,
    parts,
    own_block,
    own_coupling,
    lent_block,
    lent_coupling,
    face_list,
    eig_counts,
    owner_map,
    start_block,
):
    me = lax.axis_index("sub")
    part = lax.axis_index("face")
    faces, n, _ = own_block.shape
    held = faces * parts
    k, width = start_block.shape[1:]
    rows = faces * k
    halves = k * k // rows // parts
    group = faces * halves
    mine = lax.dynamic_slice(face_list, (me * held + part * faces, 0), (faces, 2))
    distance = (mine[:, 0] - me) % subs
    slot = (distance - 1) * faces + mine[:, 1] - part * faces
    meta = jnp.concatenate([slot, lax.dynamic_slice(eig_counts, (part * faces,), (faces,))])
    spacing = subs // 4
    owners = lax.dynamic_index_in_dim(
        owner_map.reshape(4, spacing, held), me % spacing, 1, keepdims=False
    )
    owners = jnp.repeat(owners.reshape(1, 4 * held), halves, axis=1)
    packed = (n + 16, n // 2)
    dma = pltpu.SemaphoreType.DMA
    anywhere = pl.BlockSpec(memory_space=pl.ANY)
    vmem = pl.BlockSpec(memory_space=pltpu.VMEM)
    plus = len(PLUS)
    square = pltpu.VMEM((faces, n, n), BF16)
    return pl.pallas_call(
        functools.partial(kernel, subs, parts),
        out_shape=(
            jax.ShapeDtypeStruct((held, k, width), F32),
            jax.ShapeDtypeStruct((held, k * k // parts), F32),
        ),
        in_specs=[anywhere] * 5 + [vmem, pl.BlockSpec(memory_space=pltpu.SMEM)],
        out_specs=(anywhere, vmem),
        scratch_shapes=[
            square,
            square,
            square,
            square,
            square,
            square,
            pltpu.VMEM((faces, *packed), BF16),
            pltpu.VMEM((REACH * faces, *packed), BF16),
            pltpu.VMEM((plus, *packed), BF16),
            pltpu.VMEM((parts, faces, k, width), F32),
            pltpu.VMEM((parts, faces, k, width), F32),
            pltpu.VMEM((parts, group, rows), F32),
            pltpu.VMEM((4 * parts, group, rows), F32),
            dma((4, faces)),
            dma,
            dma((faces,)),
            dma((faces,)),
            dma((plus,)),
            dma((plus,)),
            dma((faces,)),
            dma((faces,)),
            dma((faces,)),
            dma((faces,)),
            dma((faces,)),
            dma((faces,)),
            dma((parts - 1,)),
            dma((parts - 1,)),
            dma((parts - 1,)),
            dma((parts - 1,)),
            dma((4 * parts - 1,)),
            dma((4 * parts - 1,)),
        ],
        compiler_params=pltpu.CompilerParams(
            collective_id=0, has_side_effects=True, vmem_limit_bytes=48 * 1024 * 1024
        ),
    )(own_block, own_coupling, lent_block, lent_coupling, start_block, owners, meta)


def solution(mesh):
    placed = (
        P(("sub", "face"), None, None),
        P(("sub", "face"), None, None),
        P(("sub", "face"), None, None),
        P(("sub", "face"), None, None),
        P(),
        P("sub"),
        P(),
        P("sub", None, "face"),
    )
    return jax.shard_map(
        functools.partial(shards, mesh.shape["sub"], mesh.shape["face"]),
        mesh=mesh,
        in_specs=placed,
        out_specs=(P("sub", None, "face"), P("sub", "face")),
        check_vma=False,
    )
```

```python
import functools

import jax
import jax.numpy as jnp
from jax import lax
from jax.experimental import pallas as pl
from jax.experimental.pallas import tpu as pltpu
from jax.sharding import PartitionSpec as P

ITERS = 3
REACH = 4
RING = 4
RELAYED = 3
DEPTH = 2
BLOCK = 8

HIGHEST = lax.Precision.HIGHEST
MESH = pl.DeviceIdType.MESH
F32 = jnp.float32
BF16 = jnp.bfloat16


def iota(shape, dim):
    return lax.broadcasted_iota(jnp.int32, shape, dim)


def dot(a, b, ca, cb, precision=None):
    return lax.dot_general(
        a, b, (((ca,), (cb,)), ((), ())), precision=precision, preferred_element_type=F32
    )


def pack_lent(block, coupling, out_ref):
    n = block.shape[0]
    h = n // 2
    c0, c1 = coupling[:, :h], coupling[:, h:]
    b00 = block[:h, :h].astype(F32)
    b11 = block[h:, h:].astype(F32)
    row, col = iota((h, h), 0), iota((h, h), 1)
    out_ref[0:h, :] = (block[:h, h:].astype(F32) - dot(c0, c1, 0, 0)).astype(BF16)
    s00 = b00 - dot(c0, c0, 0, 0)
    s11 = b11 - dot(c1, c1, 0, 0)
    out_ref[h : 2 * h, :] = jnp.where(row <= col, s00, s11).astype(BF16)
    eye = row == col
    diagonals = [jnp.sum(jnp.where(eye, v, 0.0), axis=0, keepdims=True) for v in (s11, b00, b11)]
    at = iota((16, h), 0)
    aux = jnp.where(at == 0, diagonals[0], jnp.where(at == 1, diagonals[1], diagonals[2]))
    out_ref[2 * h :, :] = aux.astype(BF16)


def unpack_upper(packed, out_ref):
    h = packed.shape[1]
    out_ref[:h, h:] = packed
    out_ref[h:, :h] = packed.T


def unpack_mixed(packed, out_ref):
    h = packed.shape[1]
    mixed = packed[:h].astype(F32)
    aux = packed[h:].astype(F32)
    flipped = mixed.T
    row, col = iota((h, h), 0), iota((h, h), 1)
    out_ref[:h, :h] = jnp.where(row <= col, mixed, flipped).astype(BF16)
    out_ref[h:, h:] = jnp.where(
        row > col, mixed, jnp.where(row < col, flipped, aux[0:1])
    ).astype(BF16)


def kernel(
    subs,
    parts,
    own_block,
    own_coupling,
    lent_block,
    lent_coupling,
    start_block,
    face_list,
    eig_counts,
    owner_map,
    basis,
    coarse,
    lent_b,
    lent_c,
    own_b,
    own_c,
    own_s,
    lent_s,
    lent_w,
    tx,
    rx,
    passing,
    x0,
    basis_tx,
    basis_rx,
    basis_out,
    cand_tx,
    cand,
    table_s,
    count_s,
    owner_v,
    load_sem,
    index_sem,
    x0_local_sem,
    out_sem,
    lane1_send,
    lane1_recv,
    mid_send,
    mid_recv,
    lane2_send,
    lane2_recv,
    near_send,
    near_recv,
    far_send,
    far_recv,
    x0_send,
    x0_recv,
    basis_send,
    basis_recv,
    cand_send,
    cand_recv,
):
    faces = own_b.shape[0]
    n = own_b.shape[1]
    k = start_block.shape[1]
    width = start_block.shape[2]
    me = lax.axis_index("sub")
    part = lax.axis_index("face")
    core = lax.rem(me, 2)
    x = lax.rem(me // 2, RING)
    line = me - 2 * x - core
    ahead = line + 2 * lax.rem(x + 1, RING) + core
    behind = line + 2 * lax.rem(x + RING - 1, RING) + core
    spacing = subs // 4
    residue = lax.rem(me, spacing)
    turn = me // spacing

    def around(s):
        return lax.rem(s + 2 * subs, subs)

    other = me + 1 - 2 * core
    down = around(me - 2)
    up = around(me + 2)
    onward = around(behind - 4)
    top = around(me + 4)
    top_core = lax.rem(top, 2)
    top_x = lax.rem(top // 2, RING)
    feeder = top - 2 * top_x + 2 * lax.rem(top_x + 1, RING)

    loads = []
    for f in range(faces):
        for a, (src, dst) in enumerate(((lent_coupling, lent_c), (lent_block, lent_b))):
            loads.append(pltpu.make_async_copy(src.at[f], dst.at[f], load_sem.at[a, f]))
    for f in range(faces):
        for a, (src, dst) in enumerate(((own_coupling, own_c), (own_block, own_b))):
            loads.append(pltpu.make_async_copy(src.at[f], dst.at[f], load_sem.at[a + 2, f]))
    for copy in loads:
        copy.start()
    x0_local = pltpu.make_async_copy(
        start_block.at[pl.ds(part * faces, faces)], x0.at[part], x0_local_sem
    )
    x0_local.start()
    indices = [
        pltpu.make_async_copy(src, dst, index_sem.at[i])
        for i, (src, dst) in enumerate(
            ((face_list, table_s), (eig_counts, count_s), (owner_map, owner_v))
        )
    ]
    for copy in indices:
        copy.start()

    def remote(src, dst, send, recv, s, p):
        return pltpu.make_async_remote_copy(
            src_ref=src,
            dst_ref=dst,
            send_sem=send,
            recv_sem=recv,
            device_id=(s, p),
            device_id_type=MESH,
        )

    barrier = pltpu.get_barrier_semaphore()
    greeted = [(s, part) for s in (down, up, ahead, behind, onward, feeder, other)]
    peers = []
    for dk in range(4):
        for dp in range(parts):
            if dk or dp:
                s = residue + spacing * lax.rem(turn + dk, 4)
                p = lax.rem(part + dp, parts)
                peers.append((dk, dp, s, p))
                greeted.append((s, p))
    for s, p in greeted:
        pl.semaphore_signal(barrier, inc=1, device_id=(s, p), device_id_type=MESH)

    x0_copies = []
    for dp in range(1, parts):
        p = lax.rem(part + dp, parts)
        x0_copies.append(
            remote(
                start_block.at[pl.ds(p * faces, faces)],
                x0.at[part],
                x0_send.at[dp - 1],
                x0_recv.at[dp - 1],
                me,
                p,
            )
        )
    h = n // 2
    chunks = [(f, c) for f in range(faces) for c in range(2)]
    spans = (pl.ds(0, h), pl.ds(h, h + 16))
    heights = (h, h + 16)

    def half(ref, slot, c):
        return ref.at[slot, spans[c]]

    lane1, mid, lane2 = [], [], []
    for i, (f, c) in enumerate(chunks):
        here, one, two = half(tx, f, c), half(rx, faces + f, c), half(rx, 3 * faces + f, c)
        lane1.append(remote(here, one, lane1_send.at[i], lane1_recv.at[i], down, part))
        if i >= RELAYED:
            m = i - RELAYED
            through = passing.at[m, pl.ds(0, heights[c])]
            mid.append(remote(here, through, mid_send.at[m], mid_recv.at[m], ahead, part))
            lane2.append(remote(through, two, lane2_send.at[i], lane2_recv.at[i], onward, part))
        else:
            lane2.append(remote(one, two, lane2_send.at[i], lane2_recv.at[i], down, part))

    def near(i, ref, slot):
        f, c = chunks[i]
        return remote(
            half(ref, slot, c), half(rx, f, c), near_send.at[i], near_recv.at[i], other, part
        )

    def far(i, slot):
        f, c = chunks[i]
        return remote(
            half(rx, slot, c),
            half(rx, 2 * faces + f, c),
            far_send.at[i],
            far_recv.at[i],
            other,
            part,
        )

    def unpack(i, reach):
        f, c = chunks[i]
        slot = (reach - 1) * faces + f
        packed = rx[slot, spans[c]]
        if c == 0:
            unpack_upper(packed, lent_s.at[slot])
        else:
            unpack_mixed(packed, lent_s.at[slot])
            aux = packed[h:].astype(F32)
            lent_w[slot] = jnp.concatenate([aux[1:2], aux[2:3]], axis=1)

    count = len(chunks)
    passed = count - RELAYED
    minus = lane1 + lane2[:RELAYED]
    minus_from = [None] * count + lane1[:RELAYED]
    plus = mid + lane2[RELAYED:]
    plus_from = [None] * passed + mid
    arrived = []

    def receive(copy):
        if not any(copy is c for c in arrived):
            arrived.append(copy)
            copy.wait_recv()

    def start_slot(t):
        for side, needs, depth in ((minus, minus_from, DEPTH), (plus, plus_from, passed)):
            if 0 <= t - depth < len(side):
                side[t - depth].wait_send()
            if depth <= t < len(side):
                if needs[t] is not None:
                    receive(needs[t])
                side[t].start()

    for f in range(faces):
        loads[2 * f].wait()
        loads[2 * f + 1].wait()
        pack_lent(lent_b[f], lent_c[f], tx.at[f])
        if f == 0:
            pl.semaphore_wait(barrier, len(greeted))
        for t in range(2 * f, min(2 * f + 2, DEPTH)):
            lane1[t].start()
        for t in range(2 * f, 2 * f + 2):
            if t >= RELAYED:
                mid[t - RELAYED].start()

        @pl.when(core == 1)
        def _():
            for i in (2 * f, 2 * f + 1):
                near(i, tx, f).start()

    for copy in x0_copies:
        copy.start()

    own_weights = []
    eye = iota((n, n), 0) == iota((n, n), 1)
    for f in range(faces):
        loads[2 * faces + 2 * f].wait()
        loads[2 * faces + 2 * f + 1].wait()
        coupling = own_c[f]
        block = own_b[f].astype(F32)
        own_s[f] = (block - dot(coupling, coupling, 0, 0)).astype(BF16)
        own_weights.append(jnp.sum(jnp.where(eye, block, 0.0), axis=0, keepdims=True))

    def split(value):
        high = value.astype(BF16)
        return high, (value - high.astype(F32)).astype(BF16)

    def face_rows(value, f):
        return value[f * k : (f + 1) * k]

    def apply(value, tables):
        high, low = split(value)
        out = []
        for f in range(faces):
            stacked = jnp.concatenate([face_rows(high, f), face_rows(low, f)], axis=0)
            got = sum(dot(stacked, table(f), 1, 0) for table in tables)
            out.append(got[:k] + got[k:])
        return jnp.concatenate(out, axis=0)

    def slot_of(copy):
        return next(t for side in (minus, plus) for t, c in enumerate(side) if c is copy)

    last = max(len(minus), len(plus))
    tasks = {}
    for i, (f, c) in enumerate(chunks):
        two = slot_of(lane2[i])
        for t, task in (
            (i + DEPTH, "one"),
            (i + DEPTH + 2, "near"),
            (two + DEPTH, "two"),
            (two + DEPTH + 2, "far"),
        ):
            tasks.setdefault(t, []).append((i, task))
    for t in range(DEPTH, last + passed + 3):
        if t < max(len(minus) + DEPTH, len(plus) + passed):
            start_slot(t)
        if t == DEPTH + 2:
            x0_local.wait()
            for copy in x0_copies:
                copy.wait_recv()
            iterate = jnp.concatenate(
                [x0[p].reshape(faces * k, width) for p in range(parts)], axis=1
            )
            applied = apply(iterate, (own_s.__getitem__,))
        for i, task in tasks.get(t, ()):
            f, c = chunks[i]
            if task == "one":
                receive(lane1[i])

                @pl.when(core == 0)
                def _():
                    near(i, rx, faces + f).start()

                @pl.when(core == 1)
                def _():
                    far(i, faces + f).start()

                unpack(i, 2)
            elif task == "near":
                near(i, tx, 0).wait_recv()
                unpack(i, 1)
            elif task == "two":
                receive(lane2[i])

                @pl.when(core == 0)
                def _():
                    far(i, 3 * faces + f).start()

                unpack(i, 4)
            else:
                far(i, 0).wait_recv()
                unpack(i, 3)

    for copy in indices:
        copy.wait()
    slots, weight_rows = [], []
    for f in range(faces):
        at = me * faces * parts + part * faces + f
        distance = lax.rem(table_s[0, at] - me + subs, subs)
        slot = (distance - 1) * faces + table_s[1, at] - part * faces
        slots.append(jnp.clip(slot, 0, REACH * faces - 1))
        weight_rows.append(own_weights[f] + lent_w[slots[f]])
    weight = jnp.concatenate([jnp.broadcast_to(w, (k, n)) for w in weight_rows], axis=0)

    def lent(f):
        return lent_s[slots[f]]

    rows = faces * k
    lane_face = iota((rows, rows), 1) // k
    same_face = iota((rows, rows), 0) // k == lane_face
    side = (k, rows)
    row_at, lane_at = iota(side, 0), iota(side, 1)
    lane_base = lane_at // k * k

    def inverse_factor(applied, image):
        gram = jnp.where(same_face, dot(applied, image, 1, 1, HIGHEST), 0.0)
        gram = sum(face_rows(gram, f) for f in range(faces))
        inverse = jnp.where(row_at == lane_at - lane_base, 1.0, 0.0)
        pivots = jnp.ones(side, F32)
        for j in range(0, k, BLOCK):
            columns = [
                jnp.take_along_axis(gram, lane_base + j + i, axis=1, mode="promise_in_bounds")
                for i in range(BLOCK)
            ]
            gram_rows = [gram[j + i : j + i + 1] for i in range(BLOCK)]
            inverse_rows = [inverse[j + i : j + i + 1] for i in range(BLOCK)]
            for i in range(BLOCK):
                at = j + i
                pivot = columns[i][at : at + 1]
                factor = jnp.where(row_at > at, columns[i] * (1.0 / pivot), 0.0)
                pivots = jnp.where(row_at == at, pivot, pivots)
                for later in range(i + 1, BLOCK):
                    columns[later] = columns[later] - factor * columns[later][at : at + 1]
                    scale = factor[j + later : j + later + 1]
                    gram_rows[later] = gram_rows[later] - scale * gram_rows[i]
                    inverse_rows[later] = inverse_rows[later] - scale * inverse_rows[i]
                gram = gram - factor * gram_rows[i]
                inverse = inverse - factor * inverse_rows[i]
        return inverse * lax.rsqrt(pivots)

    applied = applied + apply(iterate, (lent,))
    for sweep in range(ITERS):
        image = applied / weight
        applied_next = apply(image, (own_s.__getitem__, lent))
        inverse = inverse_factor(applied, image)
        repeated = jnp.concatenate([inverse] * faces, axis=0)
        spread = jnp.where(same_face, repeated, 0.0)
        if sweep < ITERS - 1:
            applied = dot(spread, applied_next, 1, 0, HIGHEST)
    iterate = dot(spread, image, 1, 0, HIGHEST)

    face_of_row = iota((rows, 1), 0) // k
    counts = jnp.zeros((rows, 1), jnp.int32)
    for f in range(faces):
        counts = jnp.where(face_of_row == f, count_s[part * faces + f], counts)
    kept_row = iota((rows, 1), 0) - face_of_row * k < counts
    basis_rows = jnp.where(kept_row, iterate, 0.0)
    for p in range(parts):
        basis_tx[p] = (
            basis_rows[:, p * width : (p + 1) * width].reshape(faces, k, width).astype(BF16)
        )
    basis_copies = []
    for dp in range(1, parts):
        p = lax.rem(part + dp, parts)
        basis_copies.append(
            remote(
                basis_tx.at[p],
                basis_rx.at[part],
                basis_send.at[dp - 1],
                basis_recv.at[dp - 1],
                me,
                p,
            )
        )
    for copy in basis_copies:
        copy.start()

    block = jnp.where(same_face, dot(image, applied_next, 1, 1, HIGHEST), 0.0)
    block = dot(spread, dot(block, repeated, 1, 1, HIGHEST), 1, 0, HIGHEST)
    lane_kept = iota((rows, rows), 1) % k < counts
    per_row = rows // k
    mine_row = iota((rows, rows), 0) % per_row == lane_face
    block = jnp.where(mine_row & kept_row & lane_kept, block, 0.0)
    halves = k // per_row // parts
    fold_rows = parts * faces * halves
    fold_at, from_at = iota((fold_rows, rows), 0), iota((fold_rows, rows), 1)
    wanted_row = (
        fold_at // halves % faces * k
        + (fold_at // (halves * faces) * halves + fold_at % halves) * per_row
    )
    fold = (from_at // per_row * per_row == wanted_row).astype(F32)
    folded = dot(fold, block, 1, 0, HIGHEST)
    group = faces * halves
    for p in range(parts):
        cand_tx[p] = folded[p * group : (p + 1) * group]
    source = turn * parts + part
    cand_copies = []
    for i, (dk, dp, s, p) in enumerate(peers):
        cand_copies.append(
            remote(cand_tx.at[p], cand.at[source], cand_send.at[i], cand_recv.at[i], s, p)
        )
    for copy in cand_copies:
        copy.start()
    cand[source] = cand_tx[part]

    total = 4 * parts * group
    held = faces * parts
    lanes = owner_v.shape[1]
    cand_of = iota(owner_v.shape, 1) // halves
    first = cand_of // held * spacing * held + residue * held
    spot = first + cand_of % held
    owners = jnp.take_along_axis(owner_v[...], spot % lanes, axis=1, mode="promise_in_bounds")
    wanted = (owners == me) & (iota(owner_v.shape, 0) == spot // lanes)
    wanted = jnp.sum(wanted.astype(F32), axis=0, keepdims=True)
    before_at, after_at = iota((total, total), 0), iota((total, total), 1)
    before = (
        (before_at % halves == 0) & (before_at // halves < after_at // halves)
    ).astype(F32)
    rank = dot(jnp.broadcast_to(wanted, (8, total)), before, 1, 0)[0:1]
    out_rows = coarse.shape[0]
    out_at, cand_at = iota((out_rows, total), 0), iota((out_rows, total), 1)
    chosen = (wanted > 0) & (rank.astype(jnp.int32) == out_at)

    basis_out[pl.ds(part * faces, faces)] = basis_tx[part].astype(F32)
    for dp in range(1, parts):
        basis_copies[dp - 1].wait_recv()
        p = lax.rem(part + parts - dp, parts)
        basis_out[pl.ds(p * faces, faces)] = basis_rx[p].astype(F32)
    out_copy = pltpu.make_async_copy(basis_out, basis, out_sem)
    out_copy.start()

    for copy in cand_copies:
        copy.wait_recv()
    candidates = cand[...].reshape(total, rows)
    for h in range(halves):
        choose = jnp.where(chosen & (cand_at % halves == h), 1.0, 0.0)
        coarse[:, h * rows : (h + 1) * rows] = dot(choose, candidates, 1, 0, HIGHEST)

    out_copy.wait()
    for copy in x0_copies + basis_copies + cand_copies:
        copy.wait_send()
    for i in range(len(chunks)):
        near(i, tx, 0).wait_send()
        far(i, 0).wait_send()


def shards(
    subs,
    parts,
    own_block,
    own_coupling,
    lent_block,
    lent_coupling,
    face_list,
    eig_counts,
    owner_map,
    start_block,
):
    faces, n, _ = own_block.shape
    held = faces * parts
    k, width = start_block.shape[1:]
    rows = faces * k
    halves = k * k // rows // parts
    group = faces * halves
    packed = (n + 16, n // 2)
    dma = pltpu.SemaphoreType.DMA
    anywhere = pl.BlockSpec(memory_space=pl.ANY)
    vmem = pl.BlockSpec(memory_space=pltpu.VMEM)
    chunks = 2 * faces
    square = pltpu.VMEM((faces, n, n), BF16)
    return pl.pallas_call(
        functools.partial(kernel, subs, parts),
        out_shape=(
            jax.ShapeDtypeStruct((held, k, width), F32),
            jax.ShapeDtypeStruct((held, k * k // parts), F32),
        ),
        in_specs=[anywhere] * 8,
        out_specs=(anywhere, vmem),
        scratch_shapes=[
            square,
            square,
            square,
            square,
            square,
            pltpu.VMEM((REACH * faces, n, n), BF16),
            pltpu.VMEM((REACH * faces, 1, n), F32),
            pltpu.VMEM((faces, *packed), BF16),
            pltpu.VMEM((REACH * faces, *packed), BF16),
            pltpu.VMEM((chunks - RELAYED, n // 2 + 16, n // 2), BF16),
            pltpu.VMEM((parts, faces, k, width), F32),
            pltpu.VMEM((parts, faces, k, width), BF16),
            pltpu.VMEM((parts, faces, k, width), BF16),
            pltpu.VMEM((held, k, width), F32),
            pltpu.VMEM((parts, group, rows), F32),
            pltpu.VMEM((4 * parts, group, rows), F32),
            pltpu.SMEM((2, held * subs), jnp.int32),
            pltpu.SMEM((held,), jnp.int32),
            pltpu.VMEM((held * subs // rows, rows), jnp.int32),
            dma((4, faces)),
            dma((3,)),
            dma,
            dma,
            dma((chunks,)),
            dma((chunks,)),
            dma((chunks - RELAYED,)),
            dma((chunks - RELAYED,)),
            dma((chunks,)),
            dma((chunks,)),
            dma((chunks,)),
            dma((chunks,)),
            dma((chunks,)),
            dma((chunks,)),
            dma((parts - 1,)),
            dma((parts - 1,)),
            dma((parts - 1,)),
            dma((parts - 1,)),
            dma((4 * parts - 1,)),
            dma((4 * parts - 1,)),
        ],
        compiler_params=pltpu.CompilerParams(
            collective_id=0, has_side_effects=True, vmem_limit_bytes=60 * 1024 * 1024
        ),
    )(
        own_block,
        own_coupling,
        lent_block,
        lent_coupling,
        start_block,
        face_list.T,
        eig_counts,
        owner_map.reshape(held * subs // rows, rows),
    )


def solution(mesh):
    placed = (
        P(("sub", "face"), None, None),
        P(("sub", "face"), None, None),
        P(("sub", "face"), None, None),
        P(("sub", "face"), None, None),
        P(),
        P("sub"),
        P(),
        P("sub", None, "face"),
    )
    return jax.shard_map(
        functools.partial(shards, mesh.shape["sub"], mesh.shape["face"]),
        mesh=mesh,
        in_specs=placed,
        out_specs=(P("sub", None, "face"), P("sub", "face")),
        check_vma=False,
    )
```

```python
import functools

import jax
import jax.numpy as jnp
from jax import lax
from jax.experimental import pallas as pl
from jax.experimental.pallas import tpu as pltpu
from jax.sharding import PartitionSpec as P

ITERS = 3
REACH = 4
RING = 4
RELAYED = 3
DEPTH = 2
BLOCK = 8

HIGHEST = lax.Precision.HIGHEST
MESH = pl.DeviceIdType.MESH
F32 = jnp.float32
BF16 = jnp.bfloat16


def iota(shape, dim):
    return lax.broadcasted_iota(jnp.int32, shape, dim)


def dot(a, b, ca, cb, precision=None):
    return lax.dot_general(
        a, b, (((ca,), (cb,)), ((), ())), precision=precision, preferred_element_type=F32
    )


def pack_upper(block, coupling, out_ref):
    h = block.shape[0] // 2
    product = dot(coupling[:, :h], coupling[:, h:], 0, 0)
    out_ref[0:h, :] = (block[:h, h:].astype(F32) - product).astype(BF16)


def pack_mixed(block, coupling, out_ref):
    h = block.shape[0] // 2
    c0, c1 = coupling[:, :h], coupling[:, h:]
    b00 = block[:h, :h].astype(F32)
    b11 = block[h:, h:].astype(F32)
    row, col = iota((h, h), 0), iota((h, h), 1)
    s00 = b00 - dot(c0, c0, 0, 0)
    s11 = b11 - dot(c1, c1, 0, 0)
    out_ref[h : 2 * h, :] = jnp.where(row <= col, s00, s11).astype(BF16)
    eye = row == col
    diagonals = [jnp.sum(jnp.where(eye, v, 0.0), axis=0, keepdims=True) for v in (s11, b00, b11)]
    at = iota((16, h), 0)
    aux = jnp.where(at == 0, diagonals[0], jnp.where(at == 1, diagonals[1], diagonals[2]))
    out_ref[2 * h :, :] = aux.astype(BF16)


def unpack_upper(packed, out_ref):
    h = packed.shape[1]
    out_ref[:h, h:] = packed
    out_ref[h:, :h] = packed.T


def unpack_mixed(packed, out_ref):
    h = packed.shape[1]
    mixed = packed[:h].astype(F32)
    aux = packed[h:].astype(F32)
    flipped = mixed.T
    row, col = iota((h, h), 0), iota((h, h), 1)
    out_ref[:h, :h] = jnp.where(row <= col, mixed, flipped).astype(BF16)
    out_ref[h:, h:] = jnp.where(
        row > col, mixed, jnp.where(row < col, flipped, aux[0:1])
    ).astype(BF16)


def kernel(
    subs,
    parts,
    own_block,
    own_coupling,
    lent_block,
    lent_coupling,
    start_block,
    face_list,
    eig_counts,
    owner_map,
    basis_rx,
    cand,
    choose_out,
    lent_b,
    lent_c,
    own_b,
    own_c,
    own_s,
    lent_s,
    lent_w,
    tx,
    rx,
    passing,
    x0,
    basis_tx,
    block_v,
    cand_tx,
    table_s,
    count_s,
    owner_v,
    load_sem,
    index_sem,
    x0_local_sem,
    out_sem,
    lane1_send,
    lane1_recv,
    mid_send,
    mid_recv,
    lane2_send,
    lane2_recv,
    near_send,
    near_recv,
    far_send,
    far_recv,
    x0_send,
    x0_recv,
    basis_send,
    basis_recv,
    cand_send,
    cand_recv,
):
    faces = own_b.shape[0]
    n = own_b.shape[1]
    k = start_block.shape[1]
    width = start_block.shape[2]
    me = lax.axis_index("sub")
    part = lax.axis_index("face")
    core = lax.rem(me, 2)
    x = lax.rem(me // 2, RING)
    line = me - 2 * x - core
    ahead = line + 2 * lax.rem(x + 1, RING) + core
    behind = line + 2 * lax.rem(x + RING - 1, RING) + core
    spacing = subs // 4
    residue = lax.rem(me, spacing)
    turn = me // spacing

    def around(s):
        return lax.rem(s + 2 * subs, subs)

    other = me + 1 - 2 * core
    down = around(me - 2)
    up = around(me + 2)
    onward = around(behind - 4)
    top = around(me + 4)
    top_core = lax.rem(top, 2)
    top_x = lax.rem(top // 2, RING)
    feeder = top - 2 * top_x + 2 * lax.rem(top_x + 1, RING)

    loads = []
    for f in range(faces):
        for a, (src, dst) in enumerate(((lent_coupling, lent_c), (lent_block, lent_b))):
            loads.append(pltpu.make_async_copy(src.at[f], dst.at[f], load_sem.at[a, f]))
    for f in range(faces):
        for a, (src, dst) in enumerate(((own_coupling, own_c), (own_block, own_b))):
            loads.append(pltpu.make_async_copy(src.at[f], dst.at[f], load_sem.at[a + 2, f]))
    for copy in loads[:2]:
        copy.start()
    x0_local = pltpu.make_async_copy(
        start_block.at[pl.ds(part * faces, faces)], x0.at[part], x0_local_sem
    )
    indices = [
        pltpu.make_async_copy(src, dst, index_sem.at[i])
        for i, (src, dst) in enumerate(
            ((face_list, table_s), (eig_counts, count_s), (owner_map, owner_v))
        )
    ]

    def remote(src, dst, send, recv, s, p):
        return pltpu.make_async_remote_copy(
            src_ref=src,
            dst_ref=dst,
            send_sem=send,
            recv_sem=recv,
            device_id=(s, p),
            device_id_type=MESH,
        )

    barrier = pltpu.get_barrier_semaphore()
    greeted = [(s, part) for s in (down, up, ahead, behind, onward, feeder, other)]
    peers = []
    for dk in range(4):
        for dp in range(parts):
            if dk or dp:
                s = residue + spacing * lax.rem(turn + dk, 4)
                p = lax.rem(part + dp, parts)
                peers.append((dk, dp, s, p))
                greeted.append((s, p))
    for s, p in greeted:
        pl.semaphore_signal(barrier, inc=1, device_id=(s, p), device_id_type=MESH)

    x0_copies = []
    for dp in range(1, parts):
        p = lax.rem(part + dp, parts)
        x0_copies.append(
            remote(
                start_block.at[pl.ds(p * faces, faces)],
                x0.at[part],
                x0_send.at[dp - 1],
                x0_recv.at[dp - 1],
                me,
                p,
            )
        )
    h = n // 2
    chunks = [(f, c) for f in range(faces) for c in range(2)]
    spans = (pl.ds(0, h), pl.ds(h, h + 16))
    heights = (h, h + 16)

    def half(ref, slot, c):
        return ref.at[slot, spans[c]]

    lane1, mid, lane2 = [], [], []
    for i, (f, c) in enumerate(chunks):
        here, one, two = half(tx, f, c), half(rx, faces + f, c), half(rx, 3 * faces + f, c)
        lane1.append(remote(here, one, lane1_send.at[i], lane1_recv.at[i], down, part))
        if i >= RELAYED:
            m = i - RELAYED
            through = passing.at[m, pl.ds(0, heights[c])]
            mid.append(remote(here, through, mid_send.at[m], mid_recv.at[m], ahead, part))
            lane2.append(remote(through, two, lane2_send.at[i], lane2_recv.at[i], onward, part))
        else:
            lane2.append(remote(one, two, lane2_send.at[i], lane2_recv.at[i], down, part))

    def near(i, ref, slot):
        f, c = chunks[i]
        return remote(
            half(ref, slot, c), half(rx, f, c), near_send.at[i], near_recv.at[i], other, part
        )

    def far(i, slot):
        f, c = chunks[i]
        return remote(
            half(rx, slot, c),
            half(rx, 2 * faces + f, c),
            far_send.at[i],
            far_recv.at[i],
            other,
            part,
        )

    def unpack(i, reach):
        f, c = chunks[i]
        slot = (reach - 1) * faces + f
        packed = rx[slot, spans[c]]
        if c == 0:
            unpack_upper(packed, lent_s.at[slot])
        else:
            unpack_mixed(packed, lent_s.at[slot])
            aux = packed[h:].astype(F32)
            lent_w[slot] = jnp.concatenate([aux[1:2], aux[2:3]], axis=1)

    count = len(chunks)
    passed = count - RELAYED
    minus = lane1 + lane2[:RELAYED]
    minus_from = [None] * count + lane1[:RELAYED]
    plus = mid + lane2[RELAYED:]
    plus_from = [None] * passed + mid
    arrived = []

    def receive(copy):
        if not any(copy is c for c in arrived):
            arrived.append(copy)
            copy.wait_recv()

    def start_slot(t):
        for side, needs, depth in ((minus, minus_from, DEPTH), (plus, plus_from, passed)):
            if 0 <= t - depth < len(side):
                side[t - depth].wait_send()
            if depth <= t < len(side):
                if needs[t] is not None:
                    receive(needs[t])
                side[t].start()

    def start_half(i):
        if i < DEPTH:
            lane1[i].start()
        if i >= RELAYED:
            mid[i - RELAYED].start()

    later = (loads[2:6], loads[6:10] + indices, loads[10:13], loads[13:16] + [x0_local])
    for f in range(faces):
        loads[2 * f].wait()
        loads[2 * f + 1].wait()
        for copy in later[f]:
            copy.start()
        block, coupling = lent_b[f], lent_c[f]
        pack_upper(block, coupling, tx.at[f])
        if f == 0:
            pl.semaphore_wait(barrier, len(greeted))
        start_half(2 * f)
        pack_mixed(block, coupling, tx.at[f])
        start_half(2 * f + 1)

    for copy in x0_copies:
        copy.start()

    own_weights = []
    eye = iota((n, n), 0) == iota((n, n), 1)
    for f in range(faces):
        loads[2 * faces + 2 * f].wait()
        loads[2 * faces + 2 * f + 1].wait()
        coupling = own_c[f]
        block = own_b[f].astype(F32)
        own_s[f] = (block - dot(coupling, coupling, 0, 0)).astype(BF16)
        own_weights.append(jnp.sum(jnp.where(eye, block, 0.0), axis=0, keepdims=True))

    def split(value):
        high = value.astype(BF16)
        return high, (value - high.astype(F32)).astype(BF16)

    def face_rows(value, f):
        return value[f * k : (f + 1) * k]

    def apply(value, tables):
        high, low = split(value)
        out = []
        for f in range(faces):
            stacked = jnp.concatenate([face_rows(high, f), face_rows(low, f)], axis=0)
            got = sum(dot(stacked, table(f), 1, 0) for table in tables)
            out.append(got[:k] + got[k:])
        return jnp.concatenate(out, axis=0)

    def slot_of(copy):
        return next(t for side in (minus, plus) for t, c in enumerate(side) if c is copy)

    last = max(len(minus), len(plus))
    tasks = {}
    for i, (f, c) in enumerate(chunks):
        two = slot_of(lane2[i])
        for t, task in (
            (i + DEPTH, "one"),
            (i + DEPTH + 2, "near"),
            (two + DEPTH, "two"),
            (two + DEPTH + 2, "far"),
        ):
            tasks.setdefault(t, []).append((i, task))
    for t in range(DEPTH, last + passed + 3):
        if t < max(len(minus) + DEPTH, len(plus) + passed):
            start_slot(t)
        if t == DEPTH + 2:
            x0_local.wait()
            for copy in x0_copies:
                copy.wait_recv()
            iterate = jnp.concatenate(
                [x0[p].reshape(faces * k, width) for p in range(parts)], axis=1
            )
            applied = apply(iterate, (own_s.__getitem__,))
        for i, task in tasks.get(t, ()):
            f, c = chunks[i]
            if task == "one":
                receive(lane1[i])

                @pl.when(core == 0)
                def _():
                    near(i, rx, faces + f).start()

                @pl.when(core == 1)
                def _():
                    near(i, tx, f).start()
                    far(i, faces + f).start()

                unpack(i, 2)
            elif task == "near":
                near(i, tx, 0).wait_recv()
                unpack(i, 1)
            elif task == "two":
                receive(lane2[i])

                @pl.when(core == 0)
                def _():
                    far(i, 3 * faces + f).start()

                unpack(i, 4)
            else:
                far(i, 0).wait_recv()
                unpack(i, 3)

    for copy in indices:
        copy.wait()
    slots, weight_rows = [], []
    for f in range(faces):
        at = me * faces * parts + part * faces + f
        distance = lax.rem(table_s[0, at] - me + subs, subs)
        slot = (distance - 1) * faces + table_s[1, at] - part * faces
        slots.append(jnp.clip(slot, 0, REACH * faces - 1))
        weight_rows.append(own_weights[f] + lent_w[slots[f]])
    weight = jnp.concatenate([jnp.broadcast_to(w, (k, n)) for w in weight_rows], axis=0)

    def lent(f):
        return lent_s[slots[f]]

    rows = faces * k
    lane_face = iota((rows, rows), 1) // k
    same_face = iota((rows, rows), 0) // k == lane_face
    side = (k, rows)
    row_at, lane_at = iota(side, 0), iota(side, 1)
    lane_base = lane_at // k * k

    def inverse_factor(applied, image):
        gram = jnp.where(same_face, dot(applied, image, 1, 1, HIGHEST), 0.0)
        gram = sum(face_rows(gram, f) for f in range(faces))
        inverse = jnp.where(row_at == lane_at - lane_base, 1.0, 0.0)
        pivots = jnp.ones(side, F32)
        for j in range(0, k, BLOCK):
            columns = [
                jnp.take_along_axis(gram, lane_base + j + i, axis=1, mode="promise_in_bounds")
                for i in range(BLOCK)
            ]
            gram_rows = [gram[j + i : j + i + 1] for i in range(BLOCK)]
            inverse_rows = [inverse[j + i : j + i + 1] for i in range(BLOCK)]
            for i in range(BLOCK):
                at = j + i
                pivot = columns[i][at : at + 1]
                factor = jnp.where(row_at > at, columns[i] * (1.0 / pivot), 0.0)
                pivots = jnp.where(row_at == at, pivot, pivots)
                for later in range(i + 1, BLOCK):
                    columns[later] = columns[later] - factor * columns[later][at : at + 1]
                    scale = factor[j + later : j + later + 1]
                    gram_rows[later] = gram_rows[later] - scale * gram_rows[i]
                    inverse_rows[later] = inverse_rows[later] - scale * inverse_rows[i]
                gram = gram - factor * gram_rows[i]
                inverse = inverse - factor * inverse_rows[i]
        return inverse * lax.rsqrt(pivots)

    applied = applied + apply(iterate, (lent,))
    for sweep in range(ITERS):
        image = applied / weight
        applied_next = apply(image, (own_s.__getitem__, lent))
        inverse = inverse_factor(applied, image)
        repeated = jnp.concatenate([inverse] * faces, axis=0)
        spread = jnp.where(same_face, repeated, 0.0)
        if sweep < ITERS - 1:
            applied = dot(spread, applied_next, 1, 0, HIGHEST)
    iterate = dot(spread, image, 1, 0, HIGHEST)

    face_of_row = iota((rows, 1), 0) // k
    counts = jnp.zeros((rows, 1), jnp.int32)
    for f in range(faces):
        counts = jnp.where(face_of_row == f, count_s[part * faces + f], counts)
    kept_row = iota((rows, 1), 0) - face_of_row * k < counts
    basis_rows = jnp.where(kept_row, iterate, 0.0)
    for p in range(parts):
        basis_tx[p] = (
            basis_rows[:, p * width : (p + 1) * width].reshape(faces, k, width).astype(BF16)
        )
    basis_copies = []
    for dp in range(1, parts):
        p = lax.rem(part + dp, parts)
        basis_copies.append(
            remote(
                basis_tx.at[p],
                basis_rx.at[part],
                basis_send.at[dp - 1],
                basis_recv.at[dp - 1],
                me,
                p,
            )
        )
    for copy in basis_copies:
        copy.start()

    block = jnp.where(same_face, dot(image, applied_next, 1, 1, HIGHEST), 0.0)
    block = dot(spread, dot(block, repeated, 1, 1, HIGHEST), 1, 0, HIGHEST)
    lane_kept = iota((rows, rows), 1) % k < counts
    per_row = rows // k
    mine_row = iota((rows, rows), 0) % per_row == lane_face
    block = jnp.where(mine_row & kept_row & lane_kept, block, 0.0)
    block_v[...] = block
    folded = sum(block_v[pl.ds(i, k, stride=per_row), :] for i in range(per_row))
    halves = k // per_row // parts
    group = faces * halves
    for p in range(parts):
        for f in range(faces):
            at = f * k // per_row + p * halves
            cand_tx[p, f * halves : (f + 1) * halves] = folded[at : at + halves]
    source = turn * parts + part
    cand_copies = []
    for i, (dk, dp, s, p) in enumerate(peers):
        cand_copies.append(
            remote(cand_tx.at[p], cand.at[source], cand_send.at[i], cand_recv.at[i], s, p)
        )
    for copy in cand_copies:
        copy.start()
    own_copies = [
        pltpu.make_async_copy(basis_tx.at[part], basis_rx.at[part], out_sem.at[0]),
        pltpu.make_async_copy(cand_tx.at[part], cand.at[source], out_sem.at[1]),
    ]
    for copy in own_copies:
        copy.start()

    total = 4 * parts * group
    held = faces * parts
    lanes = owner_v.shape[1]
    cand_of = iota(owner_v.shape, 1) // halves
    first = cand_of // held * spacing * held + residue * held
    spot = first + cand_of % held
    owners = jnp.take_along_axis(owner_v[...], spot % lanes, axis=1, mode="promise_in_bounds")
    wanted = (owners == me) & (iota(owner_v.shape, 0) == spot // lanes)
    wanted = jnp.sum(wanted.astype(F32), axis=0, keepdims=True)
    before_at, after_at = iota((total, total), 0), iota((total, total), 1)
    before = (
        (before_at % halves == 0) & (before_at // halves < after_at // halves)
    ).astype(F32)
    rank = dot(jnp.broadcast_to(wanted, (8, total)), before, 1, 0)[0:1]
    out_rows = held
    out_at, cand_at = iota((out_rows, total), 0), iota((out_rows, total), 1)
    chosen = (wanted > 0) & (rank.astype(jnp.int32) == out_at)

    choose = [jnp.where(chosen & (cand_at % halves == h), 1.0, 0.0) for h in range(halves)]
    choose_out[...] = jnp.concatenate(choose, axis=0)

    for copy in basis_copies + cand_copies:
        copy.wait_recv()
    for copy in own_copies:
        copy.wait()
    for copy in x0_copies + basis_copies + cand_copies:
        copy.wait_send()
    for i in range(len(chunks)):
        near(i, tx, 0).wait_send()
        far(i, 0).wait_send()


def finish(basis_rx, cand, choose, basis, coarse):
    basis[...] = basis_rx[...].reshape(basis.shape).astype(F32)
    rows = coarse.shape[0]
    lanes = cand.shape[2]
    placed = dot(choose[...], cand[...].reshape(choose.shape[1], lanes), 1, 0, HIGHEST)
    for h in range(coarse.shape[1] // lanes):
        coarse[:, h * lanes : (h + 1) * lanes] = placed[h * rows : (h + 1) * rows]


def shards(
    subs,
    parts,
    own_block,
    own_coupling,
    lent_block,
    lent_coupling,
    face_list,
    eig_counts,
    owner_map,
    start_block,
):
    faces, n, _ = own_block.shape
    held = faces * parts
    k, width = start_block.shape[1:]
    rows = faces * k
    halves = k * k // rows // parts
    group = faces * halves
    packed = (n + 16, n // 2)
    dma = pltpu.SemaphoreType.DMA
    anywhere = pl.BlockSpec(memory_space=pl.ANY)
    vmem = pl.BlockSpec(memory_space=pltpu.VMEM)
    chunks = 2 * faces
    square = pltpu.VMEM((faces, n, n), BF16)
    arrived = pl.pallas_call(
        functools.partial(kernel, subs, parts),
        out_shape=(
            jax.ShapeDtypeStruct((parts, faces, k, width), BF16),
            jax.ShapeDtypeStruct((4 * parts, group, rows), F32),
            jax.ShapeDtypeStruct((held * halves, 4 * parts * group), F32),
        ),
        in_specs=[anywhere] * 8,
        out_specs=(anywhere, anywhere, vmem),
        scratch_shapes=[
            square,
            square,
            square,
            square,
            square,
            pltpu.VMEM((REACH * faces, n, n), BF16),
            pltpu.VMEM((REACH * faces, 1, n), F32),
            pltpu.VMEM((faces, *packed), BF16),
            pltpu.VMEM((REACH * faces, *packed), BF16),
            pltpu.VMEM((chunks - RELAYED, n // 2 + 16, n // 2), BF16),
            pltpu.VMEM((parts, faces, k, width), F32),
            pltpu.VMEM((parts, faces, k, width), BF16),
            pltpu.VMEM((rows, rows), F32),
            pltpu.VMEM((parts, group, rows), F32),
            pltpu.SMEM((2, held * subs), jnp.int32),
            pltpu.SMEM((held,), jnp.int32),
            pltpu.VMEM((held * subs // rows, rows), jnp.int32),
            dma((4, faces)),
            dma((3,)),
            dma,
            dma((2,)),
            dma((chunks,)),
            dma((chunks,)),
            dma((chunks - RELAYED,)),
            dma((chunks - RELAYED,)),
            dma((chunks,)),
            dma((chunks,)),
            dma((chunks,)),
            dma((chunks,)),
            dma((chunks,)),
            dma((chunks,)),
            dma((parts - 1,)),
            dma((parts - 1,)),
            dma((parts - 1,)),
            dma((parts - 1,)),
            dma((4 * parts - 1,)),
            dma((4 * parts - 1,)),
        ],
        compiler_params=pltpu.CompilerParams(
            collective_id=0, has_side_effects=True, vmem_limit_bytes=60 * 1024 * 1024
        ),
    )(
        own_block,
        own_coupling,
        lent_block,
        lent_coupling,
        start_block,
        face_list.T,
        eig_counts,
        owner_map.reshape(held * subs // rows, rows),
    )
    return pl.pallas_call(
        finish,
        out_shape=(
            jax.ShapeDtypeStruct((held, k, width), F32),
            jax.ShapeDtypeStruct((held, k * k // parts), F32),
        ),
    )(*arrived)


def solution(mesh):
    placed = (
        P(("sub", "face"), None, None),
        P(("sub", "face"), None, None),
        P(("sub", "face"), None, None),
        P(("sub", "face"), None, None),
        P(),
        P("sub"),
        P(),
        P("sub", None, "face"),
    )
    return jax.shard_map(
        functools.partial(shards, mesh.shape["sub"], mesh.shape["face"]),
        mesh=mesh,
        in_specs=placed,
        out_specs=(P("sub", None, "face"), P("sub", "face")),
        check_vma=False,
    )
```

```python
import functools

import jax
import jax.numpy as jnp
from jax import lax
from jax.experimental import pallas as pl
from jax.experimental.pallas import tpu as pltpu
from jax.sharding import PartitionSpec as P

ITERS = 3
REACH = 4
RING = 4
RELAYED = 3
DEPTH = 2
BLOCK = 8

HIGHEST = lax.Precision.HIGHEST
MESH = pl.DeviceIdType.MESH
F32 = jnp.float32
BF16 = jnp.bfloat16


def iota(shape, dim):
    return lax.broadcasted_iota(jnp.int32, shape, dim)


def dot(a, b, ca, cb, precision=None):
    return lax.dot_general(
        a, b, (((ca,), (cb,)), ((), ())), precision=precision, preferred_element_type=F32
    )


def split(value):
    high = value.astype(BF16)
    return high, (value - high.astype(F32)).astype(BF16)


def dot3(a, b, ca, cb):
    (ah, al), (bh, bl) = split(a), split(b)
    return dot(ah, bh, ca, cb) + (dot(ah, bl, ca, cb) + dot(al, bh, ca, cb))


def pack_upper(block, coupling, out_ref):
    h = block.shape[0] // 2
    product = dot(coupling[:, :h], coupling[:, h:], 0, 0)
    out_ref[0:h, :] = (block[:h, h:].astype(F32) - product).astype(BF16)


def pack_mixed(block, coupling, out_ref):
    h = block.shape[0] // 2
    c0, c1 = coupling[:, :h], coupling[:, h:]
    b00 = block[:h, :h].astype(F32)
    b11 = block[h:, h:].astype(F32)
    row, col = iota((h, h), 0), iota((h, h), 1)
    s00 = b00 - dot(c0, c0, 0, 0)
    s11 = b11 - dot(c1, c1, 0, 0)
    out_ref[h : 2 * h, :] = jnp.where(row <= col, s00, s11).astype(BF16)
    eye = row == col
    diagonals = [jnp.sum(jnp.where(eye, v, 0.0), axis=0, keepdims=True) for v in (s11, b00, b11)]
    at = iota((16, h), 0)
    aux = jnp.where(at == 0, diagonals[0], jnp.where(at == 1, diagonals[1], diagonals[2]))
    out_ref[2 * h :, :] = aux.astype(BF16)


def unpack_upper(packed, out_ref):
    h = packed.shape[1]
    out_ref[:h, h:] = packed
    out_ref[h:, :h] = packed.T


def unpack_mixed(packed, out_ref):
    h = packed.shape[1]
    mixed = packed[:h].astype(F32)
    aux = packed[h:].astype(F32)
    flipped = mixed.T
    row, col = iota((h, h), 0), iota((h, h), 1)
    out_ref[:h, :h] = jnp.where(row <= col, mixed, flipped).astype(BF16)
    out_ref[h:, h:] = jnp.where(
        row > col, mixed, jnp.where(row < col, flipped, aux[0:1])
    ).astype(BF16)


def kernel(
    subs,
    parts,
    own_block,
    own_coupling,
    lent_block,
    lent_coupling,
    start_block,
    face_list,
    eig_counts,
    owner_map,
    basis_rx,
    cand,
    choose_out,
    lent_b,
    lent_c,
    own_b,
    own_c,
    own_s,
    lent_s,
    lent_w,
    tx,
    rx,
    passing,
    x0,
    basis_tx,
    block_v,
    cand_tx,
    table_s,
    count_s,
    owner_v,
    load_sem,
    index_sem,
    x0_local_sem,
    out_sem,
    lane1_send,
    lane1_recv,
    mid_send,
    mid_recv,
    lane2_send,
    lane2_recv,
    near_send,
    near_recv,
    far_send,
    far_recv,
    x0_send,
    x0_recv,
    basis_send,
    basis_recv,
    cand_send,
    cand_recv,
):
    faces = own_b.shape[0]
    n = own_b.shape[1]
    k = start_block.shape[1]
    width = start_block.shape[2]
    me = lax.axis_index("sub")
    part = lax.axis_index("face")
    core = lax.rem(me, 2)
    x = lax.rem(me // 2, RING)
    line = me - 2 * x - core
    ahead = line + 2 * lax.rem(x + 1, RING) + core
    behind = line + 2 * lax.rem(x + RING - 1, RING) + core
    spacing = subs // 4
    residue = lax.rem(me, spacing)
    turn = me // spacing

    def around(s):
        return lax.rem(s + 2 * subs, subs)

    other = me + 1 - 2 * core
    down = around(me - 2)
    up = around(me + 2)
    onward = around(behind - 4)
    top = around(me + 4)
    top_core = lax.rem(top, 2)
    top_x = lax.rem(top // 2, RING)
    feeder = top - 2 * top_x + 2 * lax.rem(top_x + 1, RING)

    loads = []
    for f in range(faces):
        for a, (src, dst) in enumerate(((lent_coupling, lent_c), (lent_block, lent_b))):
            loads.append(pltpu.make_async_copy(src.at[f], dst.at[f], load_sem.at[a, f]))
    for f in range(faces):
        for a, (src, dst) in enumerate(((own_coupling, own_c), (own_block, own_b))):
            loads.append(pltpu.make_async_copy(src.at[f], dst.at[f], load_sem.at[a + 2, f]))
    for copy in loads[:2]:
        copy.start()
    x0_local = pltpu.make_async_copy(
        start_block.at[pl.ds(part * faces, faces)], x0.at[part], x0_local_sem
    )
    indices = [
        pltpu.make_async_copy(src, dst, index_sem.at[i])
        for i, (src, dst) in enumerate(
            ((face_list, table_s), (eig_counts, count_s), (owner_map, owner_v))
        )
    ]

    def remote(src, dst, send, recv, s, p):
        return pltpu.make_async_remote_copy(
            src_ref=src,
            dst_ref=dst,
            send_sem=send,
            recv_sem=recv,
            device_id=(s, p),
            device_id_type=MESH,
        )

    barrier = pltpu.get_barrier_semaphore()
    greeted = [(s, part) for s in (down, up, ahead, behind, onward, feeder, other)]
    peers = []
    for dk in range(4):
        for dp in range(parts):
            if dk or dp:
                s = residue + spacing * lax.rem(turn + dk, 4)
                p = lax.rem(part + dp, parts)
                peers.append((dk, dp, s, p))
                greeted.append((s, p))
    for s, p in greeted:
        pl.semaphore_signal(barrier, inc=1, device_id=(s, p), device_id_type=MESH)

    x0_copies = []
    for dp in range(1, parts):
        p = lax.rem(part + dp, parts)
        x0_copies.append(
            remote(
                start_block.at[pl.ds(p * faces, faces)],
                x0.at[part],
                x0_send.at[dp - 1],
                x0_recv.at[dp - 1],
                me,
                p,
            )
        )
    h = n // 2
    chunks = [(f, c) for f in range(faces) for c in range(2)]
    spans = (pl.ds(0, h), pl.ds(h, h + 16))
    heights = (h, h + 16)

    def half(ref, slot, c):
        return ref.at[slot, spans[c]]

    lane1, mid, lane2 = [], [], []
    for i, (f, c) in enumerate(chunks):
        here, one, two = half(tx, f, c), half(rx, faces + f, c), half(rx, 3 * faces + f, c)
        lane1.append(remote(here, one, lane1_send.at[i], lane1_recv.at[i], down, part))
        if i >= RELAYED:
            m = i - RELAYED
            through = passing.at[m, pl.ds(0, heights[c])]
            mid.append(remote(here, through, mid_send.at[m], mid_recv.at[m], ahead, part))
            lane2.append(remote(through, two, lane2_send.at[i], lane2_recv.at[i], onward, part))
        else:
            lane2.append(remote(one, two, lane2_send.at[i], lane2_recv.at[i], down, part))

    def near(i, ref, slot):
        f, c = chunks[i]
        return remote(
            half(ref, slot, c), half(rx, f, c), near_send.at[i], near_recv.at[i], other, part
        )

    def far(i, slot):
        f, c = chunks[i]
        return remote(
            half(rx, slot, c),
            half(rx, 2 * faces + f, c),
            far_send.at[i],
            far_recv.at[i],
            other,
            part,
        )

    def unpack(i, reach):
        f, c = chunks[i]
        slot = (reach - 1) * faces + f
        packed = rx[slot, spans[c]]
        if c == 0:
            unpack_upper(packed, lent_s.at[slot])
        else:
            unpack_mixed(packed, lent_s.at[slot])
            aux = packed[h:].astype(F32)
            lent_w[slot] = jnp.concatenate([aux[1:2], aux[2:3]], axis=1)

    count = len(chunks)
    passed = count - RELAYED
    minus = lane1 + lane2[:RELAYED]
    minus_from = [None] * count + lane1[:RELAYED]
    plus = mid + lane2[RELAYED:]
    plus_from = [None] * passed + mid
    arrived = []

    def receive(copy):
        if not any(copy is c for c in arrived):
            arrived.append(copy)
            copy.wait_recv()

    def start_slot(t):
        for side, needs, depth in ((minus, minus_from, DEPTH), (plus, plus_from, passed)):
            if 0 <= t - depth < len(side):
                side[t - depth].wait_send()
            if depth <= t < len(side):
                if needs[t] is not None:
                    receive(needs[t])
                side[t].start()

    def start_half(i):
        if i < DEPTH:
            lane1[i].start()
        if i >= RELAYED:
            mid[i - RELAYED].start()

    later = (loads[2:6], loads[6:10] + indices, loads[10:13], loads[13:16] + [x0_local])
    for f in range(faces):
        loads[2 * f].wait()
        loads[2 * f + 1].wait()
        for copy in later[f]:
            copy.start()
        block, coupling = lent_b[f], lent_c[f]
        pack_upper(block, coupling, tx.at[f])
        if f == 0:
            pl.semaphore_wait(barrier, len(greeted))
        start_half(2 * f)
        pack_mixed(block, coupling, tx.at[f])
        start_half(2 * f + 1)

    for copy in x0_copies:
        copy.start()

    own_weights = []
    eye = iota((n, n), 0) == iota((n, n), 1)
    for f in range(faces):
        loads[2 * faces + 2 * f].wait()
        loads[2 * faces + 2 * f + 1].wait()
        coupling = own_c[f]
        block = own_b[f].astype(F32)
        own_s[f] = (block - dot(coupling, coupling, 0, 0)).astype(BF16)
        own_weights.append(jnp.sum(jnp.where(eye, block, 0.0), axis=0, keepdims=True))

    def face_rows(value, f):
        return value[f * k : (f + 1) * k]

    def apply(value, tables):
        high, low = split(value)
        out = []
        for f in range(faces):
            stacked = jnp.concatenate([face_rows(high, f), face_rows(low, f)], axis=0)
            got = sum(dot(stacked, table(f), 1, 0) for table in tables)
            out.append(got[:k] + got[k:])
        return jnp.concatenate(out, axis=0)

    def slot_of(copy):
        return next(t for side in (minus, plus) for t, c in enumerate(side) if c is copy)

    last = max(len(minus), len(plus))
    tasks = {}
    for i, (f, c) in enumerate(chunks):
        two = slot_of(lane2[i])
        for t, task in (
            (i + DEPTH, "one"),
            (i + DEPTH + 2, "near"),
            (two + DEPTH, "two"),
            (two + DEPTH + 2, "far"),
        ):
            tasks.setdefault(t, []).append((i, task))
    for t in range(DEPTH, last + passed + 3):
        if t < max(len(minus) + DEPTH, len(plus) + passed):
            start_slot(t)
        if t == DEPTH + 2:
            x0_local.wait()
            for copy in x0_copies:
                copy.wait_recv()
            iterate = jnp.concatenate(
                [x0[p].reshape(faces * k, width) for p in range(parts)], axis=1
            )
            applied = apply(iterate, (own_s.__getitem__,))
        for i, task in tasks.get(t, ()):
            f, c = chunks[i]
            if task == "one":
                receive(lane1[i])

                @pl.when(core == 0)
                def _():
                    near(i, rx, faces + f).start()

                @pl.when(core == 1)
                def _():
                    near(i, tx, f).start()
                    far(i, faces + f).start()

                unpack(i, 2)
            elif task == "near":
                near(i, tx, 0).wait_recv()
                unpack(i, 1)
            elif task == "two":
                receive(lane2[i])

                @pl.when(core == 0)
                def _():
                    far(i, 3 * faces + f).start()

                unpack(i, 4)
            else:
                far(i, 0).wait_recv()
                unpack(i, 3)

    for copy in indices:
        copy.wait()
    slots, weight_rows = [], []
    for f in range(faces):
        at = me * faces * parts + part * faces + f
        distance = lax.rem(table_s[0, at] - me + subs, subs)
        slot = (distance - 1) * faces + table_s[1, at] - part * faces
        slots.append(jnp.clip(slot, 0, REACH * faces - 1))
        weight_rows.append(own_weights[f] + lent_w[slots[f]])
    weight = jnp.concatenate([jnp.broadcast_to(w, (k, n)) for w in weight_rows], axis=0)

    def lent(f):
        return lent_s[slots[f]]

    rows = faces * k
    lane_face = iota((rows, rows), 1) // k
    same_face = iota((rows, rows), 0) // k == lane_face
    side = (k, rows)
    row_at, lane_at = iota(side, 0), iota(side, 1)
    lane_base = lane_at // k * k

    def inverse_factor(gram):
        gram = jnp.where(same_face, gram, 0.0)
        gram = sum(face_rows(gram, f) for f in range(faces))
        inverse = jnp.where(row_at == lane_at - lane_base, 1.0, 0.0)
        pivots = jnp.ones(side, F32)
        for j in range(0, k, BLOCK):
            columns = [
                jnp.take_along_axis(gram, lane_base + j + i, axis=1, mode="promise_in_bounds")
                for i in range(BLOCK)
            ]
            gram_rows = [gram[j + i : j + i + 1] for i in range(BLOCK)]
            inverse_rows = [inverse[j + i : j + i + 1] for i in range(BLOCK)]
            for i in range(BLOCK):
                at = j + i
                pivot = columns[i][at : at + 1]
                factor = jnp.where(row_at > at, columns[i] * (1.0 / pivot), 0.0)
                pivots = jnp.where(row_at == at, pivot, pivots)
                for later in range(i + 1, BLOCK):
                    columns[later] = columns[later] - factor * columns[later][at : at + 1]
                    scale = factor[j + later : j + later + 1]
                    gram_rows[later] = gram_rows[later] - scale * gram_rows[i]
                    inverse_rows[later] = inverse_rows[later] - scale * inverse_rows[i]
                gram = gram - factor * gram_rows[i]
                inverse = inverse - factor * inverse_rows[i]
        return inverse * lax.rsqrt(pivots)

    applied = applied + apply(iterate, (lent,))
    for sweep in range(ITERS):
        image = applied / weight
        if sweep < ITERS - 1:
            gram = dot3(applied, image, 1, 1)
        else:
            gram = dot(applied, image, 1, 1, HIGHEST)
        inverse = inverse_factor(gram)
        applied_next = apply(image, (own_s.__getitem__, lent))
        repeated = jnp.concatenate([inverse] * faces, axis=0)
        spread = jnp.where(same_face, repeated, 0.0)
        if sweep < ITERS - 1:
            applied = dot3(spread, applied_next, 1, 0)
    iterate = dot3(spread, image, 1, 0)

    face_of_row = iota((rows, 1), 0) // k
    counts = jnp.zeros((rows, 1), jnp.int32)
    for f in range(faces):
        counts = jnp.where(face_of_row == f, count_s[part * faces + f], counts)
    kept_row = iota((rows, 1), 0) - face_of_row * k < counts
    basis_rows = jnp.where(kept_row, iterate, 0.0)
    for p in range(parts):
        basis_tx[p] = (
            basis_rows[:, p * width : (p + 1) * width].reshape(faces, k, width).astype(BF16)
        )
    basis_copies = []
    for dp in range(1, parts):
        p = lax.rem(part + dp, parts)
        basis_copies.append(
            remote(
                basis_tx.at[p],
                basis_rx.at[part],
                basis_send.at[dp - 1],
                basis_recv.at[dp - 1],
                me,
                p,
            )
        )
    for copy in basis_copies:
        copy.start()

    block = jnp.where(same_face, dot(image, applied_next, 1, 1, HIGHEST), 0.0)
    block = dot3(spread, dot3(block, repeated, 1, 1), 1, 0)
    lane_kept = iota((rows, rows), 1) % k < counts
    per_row = rows // k
    mine_row = iota((rows, rows), 0) % per_row == lane_face
    block = jnp.where(mine_row & kept_row & lane_kept, block, 0.0)
    block_v[...] = block
    folded = sum(block_v[pl.ds(i, k, stride=per_row), :] for i in range(per_row))
    halves = k // per_row // parts
    group = faces * halves
    for p in range(parts):
        for f in range(faces):
            at = f * k // per_row + p * halves
            cand_tx[p, f * halves : (f + 1) * halves] = folded[at : at + halves]
    source = turn * parts + part
    cand_copies = []
    for i, (dk, dp, s, p) in enumerate(peers):
        cand_copies.append(
            remote(cand_tx.at[p], cand.at[source], cand_send.at[i], cand_recv.at[i], s, p)
        )
    for copy in cand_copies:
        copy.start()
    own_copies = [
        pltpu.make_async_copy(basis_tx.at[part], basis_rx.at[part], out_sem.at[0]),
        pltpu.make_async_copy(cand_tx.at[part], cand.at[source], out_sem.at[1]),
    ]
    for copy in own_copies:
        copy.start()

    total = 4 * parts * group
    held = faces * parts
    lanes = owner_v.shape[1]
    cand_of = iota(owner_v.shape, 1) // halves
    first = cand_of // held * spacing * held + residue * held
    spot = first + cand_of % held
    owners = jnp.take_along_axis(owner_v[...], spot % lanes, axis=1, mode="promise_in_bounds")
    wanted = (owners == me) & (iota(owner_v.shape, 0) == spot // lanes)
    wanted = jnp.sum(wanted.astype(F32), axis=0, keepdims=True)
    before_at, after_at = iota((total, total), 0), iota((total, total), 1)
    before = (
        (before_at % halves == 0) & (before_at // halves < after_at // halves)
    ).astype(F32)
    rank = dot(jnp.broadcast_to(wanted, (8, total)), before, 1, 0)[0:1]
    out_rows = held
    out_at, cand_at = iota((out_rows, total), 0), iota((out_rows, total), 1)
    chosen = (wanted > 0) & (rank.astype(jnp.int32) == out_at)

    choose = [jnp.where(chosen & (cand_at % halves == h), 1.0, 0.0) for h in range(halves)]
    choose_out[...] = jnp.concatenate(choose, axis=0)

    for copy in basis_copies + cand_copies:
        copy.wait_recv()
    for copy in own_copies:
        copy.wait()
    for copy in x0_copies + basis_copies + cand_copies:
        copy.wait_send()
    for i in range(len(chunks)):
        near(i, tx, 0).wait_send()
        far(i, 0).wait_send()


def finish(basis_rx, cand, choose, basis, coarse):
    basis[...] = basis_rx[...].reshape(basis.shape).astype(F32)
    rows = coarse.shape[0]
    lanes = cand.shape[2]
    placed = dot(choose[...], cand[...].reshape(choose.shape[1], lanes), 1, 0, HIGHEST)
    for h in range(coarse.shape[1] // lanes):
        coarse[:, h * lanes : (h + 1) * lanes] = placed[h * rows : (h + 1) * rows]


def shards(
    subs,
    parts,
    own_block,
    own_coupling,
    lent_block,
    lent_coupling,
    face_list,
    eig_counts,
    owner_map,
    start_block,
):
    faces, n, _ = own_block.shape
    held = faces * parts
    k, width = start_block.shape[1:]
    rows = faces * k
    halves = k * k // rows // parts
    group = faces * halves
    packed = (n + 16, n // 2)
    dma = pltpu.SemaphoreType.DMA
    anywhere = pl.BlockSpec(memory_space=pl.ANY)
    vmem = pl.BlockSpec(memory_space=pltpu.VMEM)
    chunks = 2 * faces
    square = pltpu.VMEM((faces, n, n), BF16)
    arrived = pl.pallas_call(
        functools.partial(kernel, subs, parts),
        out_shape=(
            jax.ShapeDtypeStruct((parts, faces, k, width), BF16),
            jax.ShapeDtypeStruct((4 * parts, group, rows), F32),
            jax.ShapeDtypeStruct((held * halves, 4 * parts * group), F32),
        ),
        in_specs=[anywhere] * 8,
        out_specs=(anywhere, anywhere, vmem),
        scratch_shapes=[
            square,
            square,
            square,
            square,
            square,
            pltpu.VMEM((REACH * faces, n, n), BF16),
            pltpu.VMEM((REACH * faces, 1, n), F32),
            pltpu.VMEM((faces, *packed), BF16),
            pltpu.VMEM((REACH * faces, *packed), BF16),
            pltpu.VMEM((chunks - RELAYED, n // 2 + 16, n // 2), BF16),
            pltpu.VMEM((parts, faces, k, width), F32),
            pltpu.VMEM((parts, faces, k, width), BF16),
            pltpu.VMEM((rows, rows), F32),
            pltpu.VMEM((parts, group, rows), F32),
            pltpu.SMEM((2, held * subs), jnp.int32),
            pltpu.SMEM((held,), jnp.int32),
            pltpu.VMEM((held * subs // rows, rows), jnp.int32),
            dma((4, faces)),
            dma((3,)),
            dma,
            dma((2,)),
            dma((chunks,)),
            dma((chunks,)),
            dma((chunks - RELAYED,)),
            dma((chunks - RELAYED,)),
            dma((chunks,)),
            dma((chunks,)),
            dma((chunks,)),
            dma((chunks,)),
            dma((chunks,)),
            dma((chunks,)),
            dma((parts - 1,)),
            dma((parts - 1,)),
            dma((parts - 1,)),
            dma((parts - 1,)),
            dma((4 * parts - 1,)),
            dma((4 * parts - 1,)),
        ],
        compiler_params=pltpu.CompilerParams(
            collective_id=0, has_side_effects=True, vmem_limit_bytes=60 * 1024 * 1024
        ),
    )(
        own_block,
        own_coupling,
        lent_block,
        lent_coupling,
        start_block,
        face_list.T,
        eig_counts,
        owner_map.reshape(held * subs // rows, rows),
    )
    return pl.pallas_call(
        finish,
        out_shape=(
            jax.ShapeDtypeStruct((held, k, width), F32),
            jax.ShapeDtypeStruct((held, k * k // parts), F32),
        ),
    )(*arrived)


def solution(mesh):
    placed = (
        P(("sub", "face"), None, None),
        P(("sub", "face"), None, None),
        P(("sub", "face"), None, None),
        P(("sub", "face"), None, None),
        P(),
        P("sub"),
        P(),
        P("sub", None, "face"),
    )
    return jax.shard_map(
        functools.partial(shards, mesh.shape["sub"], mesh.shape["face"]),
        mesh=mesh,
        in_specs=placed,
        out_specs=(P("sub", None, "face"), P("sub", "face")),
        check_vma=False,
    )
```

```python
import functools

import jax
import jax.numpy as jnp
from jax import lax
from jax.experimental import pallas as pl
from jax.experimental.pallas import tpu as pltpu
from jax.sharding import PartitionSpec as P

ITERS = 3
REACH = 4
RING = 4
RELAYED = 3
DEPTH = 2
BLOCK = 8

HIGHEST = lax.Precision.HIGHEST
MESH = pl.DeviceIdType.MESH
F32 = jnp.float32
BF16 = jnp.bfloat16


def iota(shape, dim):
    return lax.broadcasted_iota(jnp.int32, shape, dim)


def dot(a, b, ca, cb, precision=None):
    return lax.dot_general(
        a, b, (((ca,), (cb,)), ((), ())), precision=precision, preferred_element_type=F32
    )


def split(value):
    high = value.astype(BF16)
    return high, (value - high.astype(F32)).astype(BF16)


def dot3(a, b, ca, cb):
    (ah, al), (bh, bl) = split(a), split(b)
    return dot(ah, bh, ca, cb) + (dot(ah, bl, ca, cb) + dot(al, bh, ca, cb))


def pack_upper(block, coupling, out_ref):
    h = block.shape[0] // 2
    product = dot(coupling[:, :h], coupling[:, h:], 0, 0)
    out_ref[0:h, :] = (block[:h, h:].astype(F32) - product).astype(BF16)


def pack_mixed(block, coupling, out_ref):
    h = block.shape[0] // 2
    c0, c1 = coupling[:, :h], coupling[:, h:]
    b00 = block[:h, :h].astype(F32)
    b11 = block[h:, h:].astype(F32)
    row, col = iota((h, h), 0), iota((h, h), 1)
    s00 = b00 - dot(c0, c0, 0, 0)
    s11 = b11 - dot(c1, c1, 0, 0)
    out_ref[h : 2 * h, :] = jnp.where(row <= col, s00, s11).astype(BF16)
    eye = row == col
    diagonals = [jnp.sum(jnp.where(eye, v, 0.0), axis=0, keepdims=True) for v in (s11, b00, b11)]
    at = iota((16, h), 0)
    aux = jnp.where(at == 0, diagonals[0], jnp.where(at == 1, diagonals[1], diagonals[2]))
    out_ref[2 * h :, :] = aux.astype(BF16)


def unpack_upper(packed, out_ref):
    h = packed.shape[1]
    out_ref[:h, h:] = packed
    out_ref[h:, :h] = packed.T


def unpack_mixed(packed, out_ref):
    h = packed.shape[1]
    mixed = packed[:h].astype(F32)
    aux = packed[h:].astype(F32)
    flipped = mixed.T
    row, col = iota((h, h), 0), iota((h, h), 1)
    out_ref[:h, :h] = jnp.where(row <= col, mixed, flipped).astype(BF16)
    out_ref[h:, h:] = jnp.where(
        row > col, mixed, jnp.where(row < col, flipped, aux[0:1])
    ).astype(BF16)


def kernel(
    subs,
    parts,
    own_block,
    own_coupling,
    lent_block,
    lent_coupling,
    start_block,
    face_list,
    eig_counts,
    owner_map,
    basis_rx,
    cand,
    choose_out,
    lent_b,
    lent_c,
    own_b,
    own_c,
    own_s,
    lent_s,
    lent_w,
    tx,
    rx,
    passing,
    x0,
    basis_tx,
    block_v,
    cand_tx,
    table_s,
    count_s,
    owner_v,
    load_sem,
    index_sem,
    x0_local_sem,
    out_sem,
    lane1_send,
    lane1_recv,
    mid_send,
    mid_recv,
    lane2_send,
    lane2_recv,
    near_send,
    near_recv,
    far_send,
    far_recv,
    x0_send,
    x0_recv,
    basis_send,
    basis_recv,
    cand_send,
    cand_recv,
):
    faces = own_b.shape[0]
    n = own_b.shape[1]
    k = start_block.shape[1]
    width = start_block.shape[2]
    me = lax.axis_index("sub")
    part = lax.axis_index("face")
    core = lax.rem(me, 2)
    x = lax.rem(me // 2, RING)
    line = me - 2 * x - core
    ahead = line + 2 * lax.rem(x + 1, RING) + core
    behind = line + 2 * lax.rem(x + RING - 1, RING) + core
    spacing = subs // 4
    residue = lax.rem(me, spacing)
    turn = me // spacing

    def around(s):
        return lax.rem(s + 2 * subs, subs)

    other = me + 1 - 2 * core
    down = around(me - 2)
    up = around(me + 2)
    onward = around(behind - 4)
    top = around(me + 4)
    top_core = lax.rem(top, 2)
    top_x = lax.rem(top // 2, RING)
    feeder = top - 2 * top_x + 2 * lax.rem(top_x + 1, RING)

    loads = []
    for f in range(faces):
        for a, (src, dst) in enumerate(((lent_coupling, lent_c), (lent_block, lent_b))):
            loads.append(pltpu.make_async_copy(src.at[f], dst.at[f], load_sem.at[a, f]))
    for f in range(faces):
        for a, (src, dst) in enumerate(((own_coupling, own_c), (own_block, own_b))):
            loads.append(pltpu.make_async_copy(src.at[f], dst.at[f], load_sem.at[a + 2, f]))
    for copy in loads[:2]:
        copy.start()
    x0_local = pltpu.make_async_copy(
        start_block.at[pl.ds(part * faces, faces)], x0.at[part], x0_local_sem
    )
    indices = [
        pltpu.make_async_copy(src, dst, index_sem.at[i])
        for i, (src, dst) in enumerate(
            ((face_list, table_s), (eig_counts, count_s), (owner_map, owner_v))
        )
    ]

    def remote(src, dst, send, recv, s, p):
        return pltpu.make_async_remote_copy(
            src_ref=src,
            dst_ref=dst,
            send_sem=send,
            recv_sem=recv,
            device_id=(s, p),
            device_id_type=MESH,
        )

    barrier = pltpu.get_barrier_semaphore()
    greeted = [(s, part) for s in (down, up, ahead, behind, onward, feeder, other)]
    peers = []
    for dk in range(4):
        for dp in range(parts):
            if dk or dp:
                s = residue + spacing * lax.rem(turn + dk, 4)
                p = lax.rem(part + dp, parts)
                peers.append((dk, dp, s, p))
                greeted.append((s, p))
    for s, p in greeted:
        pl.semaphore_signal(barrier, inc=1, device_id=(s, p), device_id_type=MESH)

    x0_copies = []
    for dp in range(1, parts):
        p = lax.rem(part + dp, parts)
        x0_copies.append(
            remote(
                start_block.at[pl.ds(p * faces, faces)],
                x0.at[part],
                x0_send.at[dp - 1],
                x0_recv.at[dp - 1],
                me,
                p,
            )
        )
    h = n // 2
    chunks = [(f, c) for f in range(faces) for c in range(2)]
    spans = (pl.ds(0, h), pl.ds(h, h + 16))
    heights = (h, h + 16)

    def half(ref, slot, c):
        return ref.at[slot, spans[c]]

    lane1, mid, lane2 = [], [], []
    for i, (f, c) in enumerate(chunks):
        here, one, two = half(tx, f, c), half(rx, faces + f, c), half(rx, 3 * faces + f, c)
        lane1.append(remote(here, one, lane1_send.at[i], lane1_recv.at[i], down, part))
        if i >= RELAYED:
            m = i - RELAYED
            through = passing.at[m, pl.ds(0, heights[c])]
            mid.append(remote(here, through, mid_send.at[m], mid_recv.at[m], ahead, part))
            lane2.append(remote(through, two, lane2_send.at[i], lane2_recv.at[i], onward, part))
        else:
            lane2.append(remote(one, two, lane2_send.at[i], lane2_recv.at[i], down, part))

    def near(i, ref, slot):
        f, c = chunks[i]
        return remote(
            half(ref, slot, c), half(rx, f, c), near_send.at[i], near_recv.at[i], other, part
        )

    def far(i, slot):
        f, c = chunks[i]
        return remote(
            half(rx, slot, c),
            half(rx, 2 * faces + f, c),
            far_send.at[i],
            far_recv.at[i],
            other,
            part,
        )

    def unpack(i, reach):
        f, c = chunks[i]
        slot = (reach - 1) * faces + f
        packed = rx[slot, spans[c]]
        if c == 0:
            unpack_upper(packed, lent_s.at[slot])
        else:
            unpack_mixed(packed, lent_s.at[slot])
            aux = packed[h:].astype(F32)
            lent_w[slot] = jnp.concatenate([aux[1:2], aux[2:3]], axis=1)

    count = len(chunks)
    passed = count - RELAYED
    minus = lane1 + lane2[:RELAYED]
    minus_from = [None] * count + lane1[:RELAYED]
    plus = mid + lane2[RELAYED:]
    plus_from = [None] * passed + mid
    arrived = []

    def receive(copy):
        if not any(copy is c for c in arrived):
            arrived.append(copy)
            copy.wait_recv()

    def start_slot(t):
        for side, needs, depth in ((minus, minus_from, DEPTH), (plus, plus_from, passed)):
            if 0 <= t - depth < len(side):
                side[t - depth].wait_send()
            if depth <= t < len(side):
                if needs[t] is not None:
                    receive(needs[t])
                side[t].start()

    def start_half(i):
        if i < DEPTH:
            lane1[i].start()
        if i >= RELAYED:
            mid[i - RELAYED].start()

    later = (loads[2:6], loads[6:10] + indices, loads[10:13], loads[13:16] + [x0_local])
    for f in range(faces):
        loads[2 * f].wait()
        loads[2 * f + 1].wait()
        for copy in later[f]:
            copy.start()
        block, coupling = lent_b[f], lent_c[f]
        pack_upper(block, coupling, tx.at[f])
        if f == 0:
            pl.semaphore_wait(barrier, len(greeted))
        start_half(2 * f)
        pack_mixed(block, coupling, tx.at[f])
        start_half(2 * f + 1)

    for copy in x0_copies:
        copy.start()

    own_weights = []
    eye = iota((n, n), 0) == iota((n, n), 1)
    for f in range(faces):
        loads[2 * faces + 2 * f].wait()
        loads[2 * faces + 2 * f + 1].wait()
        coupling = own_c[f]
        block = own_b[f].astype(F32)
        own_s[f] = (block - dot(coupling, coupling, 0, 0)).astype(BF16)
        own_weights.append(jnp.sum(jnp.where(eye, block, 0.0), axis=0, keepdims=True))

    def face_rows(value, f):
        return value[f * k : (f + 1) * k]

    def apply(value, tables):
        high, low = split(value)
        out = []
        for f in range(faces):
            stacked = jnp.concatenate([face_rows(high, f), face_rows(low, f)], axis=0)
            got = sum(dot(stacked, table(f), 1, 0) for table in tables)
            out.append(got[:k] + got[k:])
        return jnp.concatenate(out, axis=0)

    def slot_of(copy):
        return next(t for side in (minus, plus) for t, c in enumerate(side) if c is copy)

    last = max(len(minus), len(plus))
    tasks = {}
    for i, (f, c) in enumerate(chunks):
        two = slot_of(lane2[i])
        for t, task in (
            (i + DEPTH, "one"),
            (i + DEPTH + 2, "near"),
            (two + DEPTH, "two"),
            (two + DEPTH + 2, "far"),
        ):
            tasks.setdefault(t, []).append((i, task))
    for t in range(DEPTH, last + passed + 3):
        if t < max(len(minus) + DEPTH, len(plus) + passed):
            start_slot(t)
        if t == DEPTH + 2:
            x0_local.wait()
            for copy in x0_copies:
                copy.wait_recv()
            iterate = jnp.concatenate(
                [x0[p].reshape(faces * k, width) for p in range(parts)], axis=1
            )
            applied = apply(iterate, (own_s.__getitem__,))
        for i, task in tasks.get(t, ()):
            f, c = chunks[i]
            if task == "one":
                receive(lane1[i])

                @pl.when(core == 0)
                def _():
                    near(i, rx, faces + f).start()

                @pl.when(core == 1)
                def _():
                    near(i, tx, f).start()
                    far(i, faces + f).start()

                unpack(i, 2)
            elif task == "near":
                near(i, tx, 0).wait_recv()
                unpack(i, 1)
            elif task == "two":
                receive(lane2[i])

                @pl.when(core == 0)
                def _():
                    far(i, 3 * faces + f).start()

                unpack(i, 4)
            else:
                far(i, 0).wait_recv()
                unpack(i, 3)

    for copy in indices:
        copy.wait()
    slots, weight_rows = [], []
    for f in range(faces):
        at = me * faces * parts + part * faces + f
        distance = lax.rem(table_s[0, at] - me + subs, subs)
        slot = (distance - 1) * faces + table_s[1, at] - part * faces
        slots.append(jnp.clip(slot, 0, REACH * faces - 1))
        weight_rows.append(own_weights[f] + lent_w[slots[f]])
    scale = jnp.concatenate([jnp.broadcast_to(1.0 / w, (k, n)) for w in weight_rows], axis=0)

    def lent(f):
        return lent_s[slots[f]]

    rows = faces * k
    lane_face = iota((rows, rows), 1) // k
    same_face = iota((rows, rows), 0) // k == lane_face
    side = (k, rows)
    row_at, lane_at = iota(side, 0), iota(side, 1)
    lane_base = lane_at // k * k

    def inverse_factor(gram):
        gram = jnp.where(same_face, gram, 0.0)
        gram = sum(face_rows(gram, f) for f in range(faces))
        inverse = jnp.where(row_at == lane_at - lane_base, 1.0, 0.0)
        pivots = jnp.ones(side, F32)
        for j in range(0, k, BLOCK):
            columns = [
                jnp.take_along_axis(gram, lane_base + j + i, axis=1, mode="promise_in_bounds")
                for i in range(BLOCK)
            ]
            gram_rows = [gram[j + i : j + i + 1] for i in range(BLOCK)]
            inverse_rows = [inverse[j + i : j + i + 1] for i in range(BLOCK)]
            for i in range(BLOCK):
                at = j + i
                pivot = columns[i][at : at + 1]
                factor = jnp.where(row_at > at, columns[i] * (1.0 / pivot), 0.0)
                pivots = jnp.where(row_at == at, pivot, pivots)
                for later in range(i + 1, BLOCK):
                    columns[later] = columns[later] - factor * columns[later][at : at + 1]
                    scale = factor[j + later : j + later + 1]
                    gram_rows[later] = gram_rows[later] - scale * gram_rows[i]
                    inverse_rows[later] = inverse_rows[later] - scale * inverse_rows[i]
                gram = gram - factor * gram_rows[i]
                inverse = inverse - factor * inverse_rows[i]
        return inverse * lax.rsqrt(pivots)

    applied = applied + apply(iterate, (lent,))
    for sweep in range(ITERS):
        image = applied * scale
        if sweep < ITERS - 1:
            gram = dot3(applied, image, 1, 1)
        else:
            gram = dot(applied, image, 1, 1, HIGHEST)
        inverse = inverse_factor(gram)
        applied_next = apply(image, (own_s.__getitem__, lent))
        repeated = jnp.concatenate([inverse] * faces, axis=0)
        spread = jnp.where(same_face, repeated, 0.0)
        if sweep < ITERS - 1:
            applied = dot3(spread, applied_next, 1, 0)
    iterate = dot3(spread, image, 1, 0)

    face_of_row = iota((rows, 1), 0) // k
    counts = jnp.zeros((rows, 1), jnp.int32)
    for f in range(faces):
        counts = jnp.where(face_of_row == f, count_s[part * faces + f], counts)
    kept_row = iota((rows, 1), 0) - face_of_row * k < counts
    basis_rows = jnp.where(kept_row, iterate, 0.0)
    for p in range(parts):
        basis_tx[p] = (
            basis_rows[:, p * width : (p + 1) * width].reshape(faces, k, width).astype(BF16)
        )
    basis_copies = []
    for dp in range(1, parts):
        p = lax.rem(part + dp, parts)
        basis_copies.append(
            remote(
                basis_tx.at[p],
                basis_rx.at[part],
                basis_send.at[dp - 1],
                basis_recv.at[dp - 1],
                me,
                p,
            )
        )
    for copy in basis_copies:
        copy.start()

    block = jnp.where(same_face, dot3(image, applied_next, 1, 1), 0.0)
    block = dot3(spread, dot3(block, repeated, 1, 1), 1, 0)
    lane_kept = iota((rows, rows), 1) % k < counts
    per_row = rows // k
    mine_row = iota((rows, rows), 0) % per_row == lane_face
    block = jnp.where(mine_row & kept_row & lane_kept, block, 0.0)
    block_v[...] = block
    folded = sum(block_v[pl.ds(i, k, stride=per_row), :] for i in range(per_row))
    halves = k // per_row // parts
    group = faces * halves
    for p in range(parts):
        for f in range(faces):
            at = f * k // per_row + p * halves
            cand_tx[p, f * halves : (f + 1) * halves] = folded[at : at + halves]
    source = turn * parts + part
    cand_copies = []
    for i, (dk, dp, s, p) in enumerate(peers):
        cand_copies.append(
            remote(cand_tx.at[p], cand.at[source], cand_send.at[i], cand_recv.at[i], s, p)
        )
    for copy in cand_copies:
        copy.start()
    own_copies = [
        pltpu.make_async_copy(basis_tx.at[part], basis_rx.at[part], out_sem.at[0]),
        pltpu.make_async_copy(cand_tx.at[part], cand.at[source], out_sem.at[1]),
    ]
    for copy in own_copies:
        copy.start()

    total = 4 * parts * group
    held = faces * parts
    lanes = owner_v.shape[1]
    cand_of = iota(owner_v.shape, 1) // halves
    first = cand_of // held * spacing * held + residue * held
    spot = first + cand_of % held
    owners = jnp.take_along_axis(owner_v[...], spot % lanes, axis=1, mode="promise_in_bounds")
    wanted = (owners == me) & (iota(owner_v.shape, 0) == spot // lanes)
    wanted = jnp.sum(wanted.astype(F32), axis=0, keepdims=True)
    before_at, after_at = iota((total, total), 0), iota((total, total), 1)
    before = (
        (before_at % halves == 0) & (before_at // halves < after_at // halves)
    ).astype(F32)
    rank = dot(jnp.broadcast_to(wanted, (8, total)), before, 1, 0)[0:1]
    out_rows = held
    out_at, cand_at = iota((out_rows, total), 0), iota((out_rows, total), 1)
    chosen = (wanted > 0) & (rank.astype(jnp.int32) == out_at)

    choose = [jnp.where(chosen & (cand_at % halves == h), 1.0, 0.0) for h in range(halves)]
    choose_out[...] = jnp.concatenate(choose, axis=0)

    for copy in basis_copies + cand_copies:
        copy.wait_recv()
    for copy in own_copies:
        copy.wait()
    for copy in x0_copies + basis_copies + cand_copies:
        copy.wait_send()
    for i in range(len(chunks)):
        near(i, tx, 0).wait_send()
        far(i, 0).wait_send()


def finish(basis_rx, cand, choose, basis, coarse):
    basis[...] = basis_rx[...].reshape(basis.shape).astype(F32)
    rows = coarse.shape[0]
    lanes = cand.shape[2]
    high, low = split(cand[...].reshape(choose.shape[1], lanes))
    picked = choose[...].astype(BF16)
    placed = dot(picked, high, 1, 0) + dot(picked, low, 1, 0)
    for h in range(coarse.shape[1] // lanes):
        coarse[:, h * lanes : (h + 1) * lanes] = placed[h * rows : (h + 1) * rows]


def shards(
    subs,
    parts,
    own_block,
    own_coupling,
    lent_block,
    lent_coupling,
    face_list,
    eig_counts,
    owner_map,
    start_block,
):
    faces, n, _ = own_block.shape
    held = faces * parts
    k, width = start_block.shape[1:]
    rows = faces * k
    halves = k * k // rows // parts
    group = faces * halves
    packed = (n + 16, n // 2)
    dma = pltpu.SemaphoreType.DMA
    anywhere = pl.BlockSpec(memory_space=pl.ANY)
    vmem = pl.BlockSpec(memory_space=pltpu.VMEM)
    chunks = 2 * faces
    square = pltpu.VMEM((faces, n, n), BF16)
    arrived = pl.pallas_call(
        functools.partial(kernel, subs, parts),
        out_shape=(
            jax.ShapeDtypeStruct((parts, faces, k, width), BF16),
            jax.ShapeDtypeStruct((4 * parts, group, rows), F32),
            jax.ShapeDtypeStruct((held * halves, 4 * parts * group), F32),
        ),
        in_specs=[anywhere] * 8,
        out_specs=(anywhere, anywhere, vmem),
        scratch_shapes=[
            square,
            square,
            square,
            square,
            square,
            pltpu.VMEM((REACH * faces, n, n), BF16),
            pltpu.VMEM((REACH * faces, 1, n), F32),
            pltpu.VMEM((faces, *packed), BF16),
            pltpu.VMEM((REACH * faces, *packed), BF16),
            pltpu.VMEM((chunks - RELAYED, n // 2 + 16, n // 2), BF16),
            pltpu.VMEM((parts, faces, k, width), F32),
            pltpu.VMEM((parts, faces, k, width), BF16),
            pltpu.VMEM((rows, rows), F32),
            pltpu.VMEM((parts, group, rows), F32),
            pltpu.SMEM((2, held * subs), jnp.int32),
            pltpu.SMEM((held,), jnp.int32),
            pltpu.VMEM((held * subs // rows, rows), jnp.int32),
            dma((4, faces)),
            dma((3,)),
            dma,
            dma((2,)),
            dma((chunks,)),
            dma((chunks,)),
            dma((chunks - RELAYED,)),
            dma((chunks - RELAYED,)),
            dma((chunks,)),
            dma((chunks,)),
            dma((chunks,)),
            dma((chunks,)),
            dma((chunks,)),
            dma((chunks,)),
            dma((parts - 1,)),
            dma((parts - 1,)),
            dma((parts - 1,)),
            dma((parts - 1,)),
            dma((4 * parts - 1,)),
            dma((4 * parts - 1,)),
        ],
        compiler_params=pltpu.CompilerParams(
            collective_id=0, has_side_effects=True, vmem_limit_bytes=60 * 1024 * 1024
        ),
    )(
        own_block,
        own_coupling,
        lent_block,
        lent_coupling,
        start_block,
        face_list.T,
        eig_counts,
        owner_map.reshape(held * subs // rows, rows),
    )
    return pl.pallas_call(
        finish,
        out_shape=(
            jax.ShapeDtypeStruct((held, k, width), F32),
            jax.ShapeDtypeStruct((held, k * k // parts), F32),
        ),
    )(*arrived)


def solution(mesh):
    placed = (
        P(("sub", "face"), None, None),
        P(("sub", "face"), None, None),
        P(("sub", "face"), None, None),
        P(("sub", "face"), None, None),
        P(),
        P("sub"),
        P(),
        P("sub", None, "face"),
    )
    return jax.shard_map(
        functools.partial(shards, mesh.shape["sub"], mesh.shape["face"]),
        mesh=mesh,
        in_specs=placed,
        out_specs=(P("sub", None, "face"), P("sub", "face")),
        check_vma=False,
    )
```
